256 devices in a mesh: dp: 32 (over z, y_lo, core), tensor: 8 (over x, y_hi).
Axes of the slice: x: 4, y: 4 (y_hi: 2, y_lo: 2; y = y_hi * 2 + y_lo), z: 8, core: 2. Of those that a mesh axis runs over, the one named last changes fastest.
Arguments:
- layer_input: bfloat16 [4096, 8192], P('dp'), as said below
- gate_pre: bfloat16 [4096, 28672], P('dp', 'tensor'), as said below
- up_pre: bfloat16 [4096, 28672], P('dp', 'tensor'), as said below
- hidden_cot: bfloat16 [4096, 28672], P('dp', 'tensor'), as said below
- other_norms: float32 [64, 128], P('dp', 'tensor'), as said below
- noise_gate: bfloat16 [8192, 28672], P('dp', 'tensor'), may hold values from -3 to 3
Outputs:
- gate_grad: float32 [8192, 28672], P('dp', 'tensor')
The draws below stay inside these ranges and needn't reach their ends.
Inputs may be any that keep to these rules, and one draw needn't show every extreme that they name: `layer_input`: inputs of the layer, of order one. `gate_pre`: pre-activations of the gate. `up_pre`: pre-activations of the up projection. `hidden_cot`: a cotangent of the hidden units. `other_norms`: positive squared norms.
All inputs are finite; a program needn't handle non-finite values.
Results may differ from the reference program's by a relative error of at most 0.0025.
Values may be sent and summed in bfloat16 or wider, within the bound.
A program may use at most 128 MiB of HBM per device.

```python
import math
import jax
import jax.numpy as jnp
from jax import lax

D = 8192
FF = 28672
SEQ = 64
EXAMPLES = 64
OTHER = 128


cot_scale = 0.001


clip_ratio = 0.045


def blend(noise, common, weight):
    return math.sqrt(1.0 - weight) * noise + math.sqrt(weight) * common


def draw_layer_input(key, part):
    key = jax.random.fold_in(key, 5)
    key_noise, key_common = jax.random.split(key, 2)
    common = jax.random.normal(key_common, (EXAMPLES, 1, D), jnp.float32)
    noise = jax.random.normal(key_noise, (EXAMPLES, SEQ, D), jnp.float32)
    values = blend(noise, common, 0.3)
    return values.reshape(EXAMPLES * SEQ, D).astype(jnp.bfloat16)


def draw_gate_pre(key, part):
    key = jax.random.fold_in(key, 7)
    key_noise, key_common = jax.random.split(key, 2)
    common = jax.random.normal(key_common, (EXAMPLES, 1, FF), jnp.float32)
    noise = jax.random.normal(key_noise, (EXAMPLES, SEQ, FF), jnp.float32)
    values = blend(noise, common, 0.3)
    return values.reshape(EXAMPLES * SEQ, FF).astype(jnp.bfloat16)


def draw_up_pre(key, part):
    key = jax.random.fold_in(key, 9)
    key_noise, key_common = jax.random.split(key, 2)
    common = jax.random.normal(key_common, (EXAMPLES, 1, FF), jnp.float32)
    noise = jax.random.normal(key_noise, (EXAMPLES, SEQ, FF), jnp.float32)
    values = blend(noise, common, 0.3)
    return values.reshape(EXAMPLES * SEQ, FF).astype(jnp.bfloat16)


def draw_hidden_cot(key, part):
    key = jax.random.fold_in(key, 11)
    key_example, key_column, key_values, key_common, key_shared = jax.random.split(key, 5)
    example_scale = jnp.exp(jax.random.uniform(key_example, (EXAMPLES, 1, 1), jnp.float32, 0.0, math.log(10.0)))
    column_scale = jnp.exp(jax.random.uniform(key_column, (FF,), jnp.float32, 0.0, math.log(10.0)))
    column_scale = column_scale * 3.0 ** (jnp.arange(FF, dtype=jnp.float32) / FF)
    common = jax.random.normal(key_common, (EXAMPLES, 1, FF), jnp.float32)
    noise = jax.random.normal(key_values, (EXAMPLES, SEQ, FF), jnp.float32)
    values = blend(noise, common, 0.3)
    result = values * example_scale * column_scale * cot_scale
    return result.reshape(EXAMPLES * SEQ, FF).astype(jnp.bfloat16)


def draw_other_norms(key, part):
    key = jax.random.fold_in(key, 23)
    clip_bound = clip_ratio * math.sqrt(SEQ * D * FF)
    spread = jnp.exp(jax.random.uniform(key, (EXAMPLES, OTHER), jnp.float32, math.log(0.3), math.log(3.0)))
    rising = 3.0 ** (jnp.arange(OTHER, dtype=jnp.float32) / max(OTHER - 1, 1))
    return clip_bound * clip_bound * 0.25 / OTHER * spread * rising


def block_levels(key, extent, shards, smallest, top_value):
    gain = 1.0
    for position, shards_of in shards:
        draws = jax.random.uniform(jax.random.fold_in(jax.random.fold_in(key, 6), position), (shards_of,), jnp.float32, smallest / len(shards), top_value / len(shards))
        gain = gain * jnp.repeat(jnp.exp(draws), extent[position] // shards_of).reshape((-1,) + (1,) * (len(extent) - 1 - position))
    return gain


def scatter_about(own_key, dims, width, most, cuts=(), held_as=jnp.bfloat16):
    values = width * jax.random.normal(own_key, dims, jnp.float32)
    if cuts:
        values = values * block_levels(own_key, dims, cuts, -0.22, 0.18)
    return jnp.clip(values, -most, most).astype(held_as)


def setup_inputs(seed: int = 0) -> dict:
    keys = jax.random.split(jax.random.key(seed), 7)
    return {
        "layer_input": draw_layer_input(jax.random.fold_in(keys[6], 71), 0),
        "gate_pre": draw_gate_pre(jax.random.fold_in(keys[6], 71), 0),
        "up_pre": draw_up_pre(jax.random.fold_in(keys[6], 71), 0),
        "hidden_cot": draw_hidden_cot(jax.random.fold_in(keys[6], 71), 0),
        "other_norms": draw_other_norms(jax.random.fold_in(keys[6], 71), 0),
        "noise_gate": scatter_about(keys[5], (D, FF), 0.5, 3.0, ((0, 32), (1, 8))),
    }


clip_ratio = 0.045

def reference(layer_input, gate_pre, up_pre, hidden_cot, other_norms, noise_gate):
    gate = gate_pre.astype(jnp.float32)
    upper = up_pre.astype(jnp.float32)
    cotan = hidden_cot.astype(jnp.float32)
    sigmoid_gate = jax.nn.sigmoid(gate)
    activated = gate * sigmoid_gate
    slope = sigmoid_gate * (1.0 + gate * (1.0 - sigmoid_gate))
    gate_cot = (cotan * upper * slope).astype(jnp.bfloat16)
    up_cot = (cotan * activated).astype(jnp.bfloat16)

    def per_example(operands):
        inputs_e, gate_e, up_e = operands
        gram_x = jnp.dot(inputs_e, inputs_e.T, preferred_element_type=jnp.float32)
        gram_cot = jnp.dot(gate_e, gate_e.T, preferred_element_type=jnp.float32)
        gram_cot = gram_cot + jnp.dot(up_e, up_e.T, preferred_element_type=jnp.float32)
        return jnp.sum(gram_x * gram_cot)
    ghost = lax.map(per_example, (layer_input.reshape(EXAMPLES, SEQ, D), gate_cot.reshape(EXAMPLES, SEQ, FF), up_cot.reshape(EXAMPLES, SEQ, FF)))
    sq_norm = ghost + lax.optimization_barrier(jnp.sum(other_norms, axis=1))
    clip_bound = clip_ratio * math.sqrt(SEQ * D * FF)
    factor = clip_bound / jnp.maximum(jnp.sqrt(sq_norm), clip_bound)
    clipped = gate_cot.astype(jnp.float32).reshape(EXAMPLES, SEQ, FF) * factor[:, None, None]
    clipped = clipped.astype(jnp.bfloat16).reshape(EXAMPLES * SEQ, FF)
    grad = jnp.dot(layer_input.T, clipped, preferred_element_type=jnp.float32)
    return grad + noise_gate.astype(jnp.float32)
```

```python
import math

import jax
import jax.numpy as jnp
from jax import lax
from jax.experimental import pallas as pl
from jax.experimental.pallas import tpu as pltpu
from jax.sharding import PartitionSpec as P

D = 8192
FF = 28672
SEQ = 64
clip_ratio = 0.045
clip_bound = clip_ratio * math.sqrt(SEQ * D * FF)

Z = 8
Q = 4
XN = 4
T = 8
TOK = 128
COLS = 3584
PART = COLS // Q
W = 128
J = PART // W
ROWS = 1024
OWN = ROWS // Q
LANES = Z * TOK
HALF = LANES // 2
MESH = pl.DeviceIdType.MESH
f32 = jnp.float32
bf16 = jnp.bfloat16


def aligned(value, to=128):
    return pl.multiple_of(value, to)


def kernel(
    x_hbm, g_hbm, u_hbm, c_hbm, other_ref, out_ref,
    x_v, g_v, u_v, c_v, gc, uc, cb, cs, xt, xs, ob, gram, pn, fac,
    in_sem, xz_s, xz_r, xa_s, xa_r, yb_s, yb_r, ya_s, ya_r, xb_s, xb_r, co_s, co_r,
    qa_s, qa_r, rp_s, rp_r, rm_s, rm_r, pn_s, pn_r, fq_s, fq_r, fz_s, fz_r, out_s, out_r, own_s,
):
    dp = lax.axis_index("dp")
    tn = lax.axis_index("tensor")
    z, q = lax.div(dp, Q), lax.rem(dp, Q)
    ylo, core = lax.div(q, 2), lax.rem(q, 2)
    x, yhi = lax.div(tn, 2), lax.rem(tn, 2)
    yy = yhi * 2 + ylo
    xrow = aligned(x * TOK)

    def zq(zd, qd):
        return (zd * Q + qd, tn)

    def x_peer(off):
        return (dp, lax.rem(x + off, XN) * 2 + yhi)

    def y_peer(off):
        to = lax.rem(yy + off, 4)
        return (z * Q + lax.rem(to, 2) * 2 + core, x * 2 + lax.div(to, 2))

    def z_peer(off):
        return zq(lax.rem(z + off, Z), q)

    def q_peer(off):
        return zq(z, lax.rem(q + off, Q))

    def t_peer(off):
        return (dp, lax.rem(tn + off, T))

    core_peer = zq(z, ylo * 2 + 1 - core)

    def remote(src, dst, send, recv, device):
        return pltpu.make_async_remote_copy(
            src_ref=src, dst_ref=dst, send_sem=send, recv_sem=recv,
            device_id=device, device_id_type=MESH,
        )

    loads = [
        pltpu.make_async_copy(src, dst, in_sem.at[i])
        for i, (src, dst) in enumerate(((x_hbm, x_v), (g_hbm, g_v), (u_hbm, u_v), (c_hbm, c_v)))
    ]
    for load in loads:
        load.start()

    barrier = pltpu.get_barrier_semaphore()

    def greet(device):
        pl.semaphore_signal(barrier, inc=1, device_id=device, device_id_type=MESH)

    for off in range(1, Q):
        greet(q_peer(off))
    for off in range(1, Z):
        greet(z_peer(off))
    for off in range(1, T):
        greet(t_peer(off))
    greet((z * Q + (1 - ylo) * 2 + core, x * 2 + 1 - yhi))

    loads[0].wait()

    def turn(zd, _):
        at = aligned(zd * ROWS + yhi * (ROWS // 2) + x * TOK)
        xs[zd] = x_v[:, pl.ds(at, TOK)].T
        return 0

    lax.fori_loop(0, Z, turn, 0)
    mine = xt.at[yhi, pl.ds(xrow, TOK), pl.ds(aligned(q * LANES + z * TOK), TOK)]
    mine[...] = xs[z]

    pl.semaphore_wait(barrier, (Q - 1) + (Z - 1) + (T - 1) + 1)

    def x_z(off):
        return remote(xs.at[lax.rem(z + off, Z)], mine, xz_s.at[off], xz_r.at[off], z_peer(off))

    for off in range(1, Z):
        x_z(off).start()

    for load in loads[1:]:
        load.wait()

    def quad(j, off):
        to = lax.rem(q + off, Q)
        return remote(
            gc.at[:, pl.ds(aligned(to * PART + j * W), W)], cb.at[j, q, z],
            qa_s.at[j, off], qa_r.at[j, off], q_peer(off),
        )

    def cotangents(j):
        for part in range(Q):
            at = pl.ds(aligned(part * PART + j * W), W)
            gate = g_v[:, at].astype(f32)
            upper = u_v[:, at].astype(f32)
            cotan = c_v[:, at].astype(f32)
            sig = jax.nn.sigmoid(gate)
            slope = sig * (1.0 + gate * (1.0 - sig))
            gc[:, at] = (cotan * upper * slope).astype(bf16)
            uc[:, at] = (cotan * (gate * sig)).astype(bf16)
        for off in range(1, Q):
            quad(j, off).start()
        cb[j, q, z] = gc[:, pl.ds(aligned(q * PART + j * W), W)]

    def hop_plus(h, j):
        src = lax.rem(z + Z - (h - 1), Z)
        block = cb.at[j, :, src] if h < 4 else cb.at[j, pl.ds(0, 2), src]
        return remote(block, block, rp_s.at[h - 1, j], rp_r.at[h - 1, j], z_peer(1))

    def hop_minus(h, j):
        src = lax.rem(z + (h - 1), Z)
        block = cb.at[j, :, src] if h < 4 else cb.at[j, pl.ds(2, 2), src]
        return remote(block, block, rm_s.at[h - 1, j], rm_r.at[h - 1, j], z_peer(Z - 1))

    def first_hop(j):
        for off in range(1, Q):
            quad(j, off).wait_recv()
        hop_plus(1, j).start()
        hop_minus(1, j).start()

    cotangents(0)

    def produce(j, _):
        cotangents(j)
        first_hop(j - 1)
        return 0

    lax.fori_loop(1, J, produce, 0)
    first_hop(J - 1)

    cross = (((1,), (1,)), ((), ()))
    gram[...] = jnp.zeros_like(gram)

    def gram_x(k, _):
        part = x_v[:, pl.ds(aligned(k * 1024), 1024)]
        gram[0] += lax.dot_general(part, part, cross, preferred_element_type=f32)
        return 0

    lax.fori_loop(0, D // 1024, gram_x, 0)

    def gram_cot(k, _):
        at = pl.ds(aligned(k * 512), 512)
        gate, upper = gc[:, at], uc[:, at]
        gram[1] += lax.dot_general(gate, gate, cross, preferred_element_type=f32)
        gram[1] += lax.dot_general(upper, upper, cross, preferred_element_type=f32)
        return 0

    lax.fori_loop(0, COLS // 512, gram_cot, 0)

    for e in range(TOK // SEQ):
        at = slice(e * SEQ, (e + 1) * SEQ)
        ghost = jnp.sum(gram[0, at, at] * gram[1, at, at], axis=1, keepdims=True)
        ghost = jnp.sum(ghost, axis=0, keepdims=True)
        rest = jnp.sum(other_ref[e : e + 1, :], axis=1, keepdims=True)
        pn[0, e : e + 1, :] = jnp.broadcast_to(ghost + rest, (1, 128))
    pn[0, 2:8, :] = jnp.zeros((6, 128), f32)

    def norms(off):
        return remote(pn.at[0], pn.at[off], pn_s.at[off], pn_r.at[off], t_peer(off))

    for off in range(1, T):
        norms(off).start()

    def x_a(off):
        part = xt.at[yhi, pl.ds(xrow, TOK), pl.ds(aligned(q * LANES), HALF)]
        return remote(part, part, xa_s.at[off], xa_r.at[off], x_peer(off))

    def y_b(off):
        part = xt.at[yhi, pl.ds(xrow, TOK), pl.ds(aligned(q * LANES + HALF), HALF)]
        return remote(part, part, yb_s.at[off], yb_r.at[off], y_peer(off))

    def y_a(off):
        part = xt.at[yhi, :, pl.ds(aligned(q * LANES), HALF)]
        return remote(part, part, ya_s.at[off], ya_r.at[off], y_peer(off))

    def x_b(off, lo):
        part = xt.at[:, pl.ds(xrow, TOK), pl.ds(aligned((lo * 2 + core) * LANES + HALF), HALF)]
        return remote(part, part, xb_s.at[lo, off], xb_r.at[lo, off], x_peer(off))

    def swap(half, lo):
        part = xt.at[:, :, pl.ds(aligned((lo * 2 + core) * LANES + half * HALF), HALF)]
        return remote(part, part, co_s.at[half, lo], co_r.at[half, lo], core_peer)

    for off in range(1, Z):
        x_z(off).wait_recv()
    for off in range(1, XN):
        x_a(off).start()
        y_b(off).start()

    def second_hop(j, _):
        hop_plus(1, j).wait_recv()
        hop_plus(2, j).start()
        hop_minus(1, j).wait_recv()
        hop_minus(2, j).start()
        return 0

    lax.fori_loop(0, J, second_hop, 0)

    for off in range(1, T):
        norms(off).wait_recv()
    total = jnp.zeros((8, 128), f32)
    for t in range(T):
        total = total + pn[lax.rem(tn + T - t, T)]
    fac[z, q] = clip_bound / jnp.maximum(jnp.sqrt(total), clip_bound)

    def factor_q(off):
        return remote(fac.at[z, q], fac.at[z, q], fq_s.at[off], fq_r.at[off], q_peer(off))

    def factor_z(off):
        return remote(fac.at[z], fac.at[z], fz_s.at[off], fz_r.at[off], z_peer(off))

    for off in range(1, Q):
        factor_q(off).start()

    for off in range(1, XN):
        x_a(off).wait_recv()
        y_b(off).wait_recv()
    for off in range(1, XN):
        y_a(off).start()
        for lo in range(2):
            x_b(off, lo).start()

    for off in range(1, Q):
        factor_q(off).wait_recv()
    for off in range(1, Z):
        factor_z(off).start()
    for off in range(1, Z):
        factor_z(off).wait_recv()

    def scale(j, src):
        for part in range(Q):
            for e in range(TOK // SEQ):
                block = cb[j, part, src, e * SEQ : (e + 1) * SEQ, :].astype(f32)
                block = block * fac[src, part, e : e + 1, :]
                at = aligned((part * Z + src) * TOK + e * SEQ, SEQ)
                cs[j, pl.ds(at, SEQ), :] = block.astype(bf16)

    def third_hop(j, _):
        hop_plus(2, j).wait_recv()
        hop_plus(3, j).start()
        hop_minus(2, j).wait_recv()
        hop_minus(3, j).start()
        for off in (0, 1, Z - 1):
            scale(j, lax.rem(z + off, Z))
        return 0

    lax.fori_loop(0, J, third_hop, 0)

    for off in range(1, XN):
        y_a(off).wait_recv()
    for lo in range(2):
        swap(0, lo).start()
    for off in range(1, XN):
        for lo in range(2):
            x_b(off, lo).wait_recv()
    for lo in range(2):
        swap(1, lo).start()

    def fourth_hop(j, _):
        hop_plus(3, j).wait_recv()
        hop_plus(4, j).start()
        hop_minus(3, j).wait_recv()
        hop_minus(4, j).start()
        for off in (2, 3, Z - 3, Z - 2):
            scale(j, lax.rem(z + off, Z))
        return 0

    lax.fori_loop(0, J, fourth_hop, 0)

    for half in range(2):
        for lo in range(2):
            swap(half, lo).wait_recv()

    def place(j, part):
        return out_ref.at[:, pl.ds(aligned(part * PART + j * W), W)]

    def give(j, off):
        to = lax.rem(q + off, Q)
        return remote(
            ob.at[j, to], place(j, q), out_s.at[j, off], out_r.at[j, off], q_peer(off)
        )

    def keep(j):
        return pltpu.make_async_copy(ob.at[j, q], place(j, q), own_s.at[j])

    def multiply(j, _):
        hop_plus(4, j).wait_recv()
        hop_minus(4, j).wait_recv()
        scale(j, lax.rem(z + 4, Z))
        for half in range(2):
            grad = jnp.dot(xt[half], cs[j], preferred_element_type=f32).astype(bf16)
            ob[j, 2 * half] = grad[:OWN]
            ob[j, 2 * half + 1] = grad[OWN:]
        for off in range(1, Q):
            give(j, off).start()
        keep(j).start()
        return 0

    lax.fori_loop(0, J, multiply, 0)

    for off in range(1, Z):
        x_z(off).wait_send()
        factor_z(off).wait_send()
    for off in range(1, T):
        norms(off).wait_send()
    for off in range(1, Q):
        x_a(off).wait_send()
        y_b(off).wait_send()
        y_a(off).wait_send()
        for lo in range(2):
            x_b(off, lo).wait_send()
        factor_q(off).wait_send()
    for half in range(2):
        for lo in range(2):
            swap(half, lo).wait_send()

    def finish(j, _):
        for off in range(1, Q):
            quad(j, off).wait_send()
        for h in range(1, 5):
            hop_plus(h, j).wait_send()
            hop_minus(h, j).wait_send()
        for off in range(1, Q):
            give(j, off).wait_send()
            give(j, off).wait_recv()
        keep(j).wait()
        return 0

    lax.fori_loop(0, J, finish, 0)


def shards(layer_input, gate_pre, up_pre, hidden_cot, other_norms, noise_gate):
    dma = pltpu.SemaphoreType.DMA
    anywhere = pl.BlockSpec(memory_space=pl.ANY)
    grad = pl.pallas_call(
        kernel,
        out_shape=jax.ShapeDtypeStruct((OWN, COLS), bf16),
        in_specs=[anywhere] * 4 + [pl.BlockSpec(memory_space=pltpu.VMEM)],
        out_specs=anywhere,
        scratch_shapes=[
            pltpu.VMEM((TOK, D), bf16),
            pltpu.VMEM((TOK, COLS), bf16),
            pltpu.VMEM((TOK, COLS), bf16),
            pltpu.VMEM((TOK, COLS), bf16),
            pltpu.VMEM((TOK, COLS), bf16),
            pltpu.VMEM((TOK, COLS), bf16),
            pltpu.VMEM((J, Q, Z, TOK, W), bf16),
            pltpu.VMEM((J, Q * Z * TOK, W), bf16),
            pltpu.VMEM((2, ROWS // 2, Q * LANES), bf16),
            pltpu.VMEM((Z, TOK, TOK), bf16),
            pltpu.VMEM((J, Q, OWN, W), bf16),
            pltpu.VMEM((2, TOK, TOK), f32),
            pltpu.VMEM((T, 8, 128), f32),
            pltpu.VMEM((Z, Q, 8, 128), f32),
            dma((4,)),
            dma((Z,)), dma((Z,)),
            dma((4,)), dma((4,)), dma((4,)), dma((4,)), dma((4,)), dma((4,)),
            dma((2, 4)), dma((2, 4)), dma((2, 2)), dma((2, 2)),
            dma((J, Q)), dma((J, Q)),
            dma((4, J)), dma((4, J)), dma((4, J)), dma((4, J)),
            dma((T,)), dma((T,)), dma((Q,)), dma((Q,)), dma((Z,)), dma((Z,)),
            dma((J, Q)), dma((J, Q)), dma((J,)),
        ],
        compiler_params=pltpu.CompilerParams(
            collective_id=0, has_side_effects=True, vmem_limit_bytes=56 * 1024 * 1024
        ),
        cost_estimate=pl.CostEstimate(
            flops=2 * 4096 * 256 * 3584, bytes_accessed=8 * 1024 * 1024, transcendentals=128 * 3584
        ),
        name="clipped_gradient",
    )(layer_input, gate_pre, up_pre, hidden_cot, other_norms)
    return grad.astype(f32) + noise_gate.astype(f32)


def solution(mesh):
    placed = (
        P("dp", None),
        P("dp", "tensor"),
        P("dp", "tensor"),
        P("dp", "tensor"),
        P("dp", "tensor"),
        P("dp", "tensor"),
    )
    return jax.shard_map(
        shards, mesh=mesh, in_specs=placed, out_specs=P("dp", "tensor"), check_vma=False
    )
```

```python
import math

import jax
import jax.numpy as jnp
from jax import lax
from jax.experimental import pallas as pl
from jax.experimental.pallas import tpu as pltpu
from jax.sharding import PartitionSpec as P

D = 8192
FF = 28672
SEQ = 64
clip_ratio = 0.045
clip_bound = clip_ratio * math.sqrt(SEQ * D * FF)

Z = 8
Q = 4
XN = 4
T = 8
TOK = 128
COLS = 3584
PART = COLS // Q
W = 128
J = PART // W
ROWS = 1024
OWN = ROWS // Q
A, B = pl.ds(0, Z // 2), pl.ds(Z // 2, Z // 2)
LAG = 2
AHEAD = 3
MESH = pl.DeviceIdType.MESH
f32 = jnp.float32
bf16 = jnp.bfloat16


def aligned(value, to=128):
    return pl.multiple_of(value, to)


def tokens(q):
    return pl.ds(aligned(q * TOK), TOK)


def kernel(
    x_hbm, g_hbm, u_hbm, c_hbm, other_hbm, out_ref,
    x_v, g_v, u_v, c_v, other_v, gc, cb, cs, xt, xs, ob, acc, gram, pn, fac,
    in_sem, xz_s, xz_r, xa_s, xa_r, yb_s, yb_r, ya_s, ya_r, xb_s, xb_r, ca_s, ca_r, co_s, co_r,
    qa_s, qa_r, rp_s, rp_r, rm_s, rm_r, pn_s, pn_r, fq_s, fq_r, fz_s, fz_r, out_s, out_r, own_s,
):
    dp = lax.axis_index("dp")
    tn = lax.axis_index("tensor")
    z, q = lax.div(dp, Q), lax.rem(dp, Q)
    ylo, core = lax.div(q, 2), lax.rem(q, 2)
    x, yhi = lax.div(tn, 2), lax.rem(tn, 2)
    yy = yhi * 2 + ylo
    xrow = aligned(x * TOK)

    def zq(zd, qd):
        return (zd * Q + qd, tn)

    def x_peer(off):
        return (dp, lax.rem(x + off, XN) * 2 + yhi)

    def y_peer(off):
        to = lax.rem(yy + off, 4)
        return (z * Q + lax.rem(to, 2) * 2 + core, x * 2 + lax.div(to, 2))

    def z_peer(off):
        return zq(lax.rem(z + off, Z), q)

    def q_peer(off):
        return zq(z, lax.rem(q + off, Q))

    def t_peer(off):
        return (dp, lax.rem(tn + off, T))

    core_peer = zq(z, ylo * 2 + 1 - core)

    def remote(src, dst, send, recv, device):
        return pltpu.make_async_remote_copy(
            src_ref=src, dst_ref=dst, send_sem=send, recv_sem=recv,
            device_id=device, device_id_type=MESH,
        )

    loads = [
        pltpu.make_async_copy(src, dst, in_sem.at[i])
        for i, (src, dst) in enumerate(
            ((x_hbm, x_v), (g_hbm, g_v), (u_hbm, u_v), (c_hbm, c_v), (other_hbm, other_v))
        )
    ]
    for load in loads:
        load.start()

    barrier = pltpu.get_barrier_semaphore()

    def greet(device):
        pl.semaphore_signal(barrier, inc=1, device_id=device, device_id_type=MESH)

    for off in range(1, Q):
        greet(q_peer(off))
    for off in range(1, Z):
        greet(z_peer(off))
    for off in range(1, T):
        greet(t_peer(off))
    greet((z * Q + (1 - ylo) * 2 + core, x * 2 + 1 - yhi))

    def quad(j, off):
        to = lax.rem(q + off, Q)
        return remote(
            gc.at[:, pl.ds(aligned(to * PART + j * W), W)], cb.at[j, z, q],
            qa_s.at[j, off], qa_r.at[j, off], q_peer(off),
        )

    def cotangents(j):
        for part in range(Q):
            at = pl.ds(aligned(part * PART + j * W), W)
            gate = g_v[:, at].astype(f32)
            upper = u_v[:, at].astype(f32)
            cotan = c_v[:, at].astype(f32)
            sig = jax.nn.sigmoid(gate)
            slope = sig * (1.0 + gate * (1.0 - sig))
            gc[:, at] = (cotan * upper * slope).astype(bf16)

    def spread(j):
        for off in range(1, Q):
            quad(j, off).start()
        cb[j, z, q] = gc[:, pl.ds(aligned(q * PART + j * W), W)]

    def hop_plus(h, j):
        src = lax.rem(z + Z - (h - 1), Z)
        block = cb.at[j, src] if h < 4 else cb.at[j, src, pl.ds(0, 2)]
        return remote(block, block, rp_s.at[h - 1, j], rp_r.at[h - 1, j], z_peer(1))

    def hop_minus(h, j):
        src = lax.rem(z + (h - 1), Z)
        block = cb.at[j, src] if h < 4 else cb.at[j, src, pl.ds(2, 2)]
        return remote(block, block, rm_s.at[h - 1, j], rm_r.at[h - 1, j], z_peer(Z - 1))

    def first_hop(j):
        for off in range(1, Q):
            quad(j, off).wait_recv()
        hop_plus(1, j).start()
        hop_minus(1, j).start()

    def next_hop(h, j):
        hop_plus(h - 1, j).wait_recv()
        hop_plus(h, j).start()
        hop_minus(h - 1, j).wait_recv()
        hop_minus(h, j).start()

    def turn(zd, _):
        at = aligned(zd * ROWS + yhi * (ROWS // 2) + x * TOK)
        xs[zd] = x_v[:, pl.ds(at, TOK)].T
        return 0

    mine = xt.at[z, yhi, pl.ds(xrow, TOK), tokens(q)]

    def x_z(off):
        return remote(xs.at[lax.rem(z + off, Z)], mine, xz_s.at[off], xz_r.at[off], z_peer(off))

    loads[0].wait()
    lax.fori_loop(0, Z, turn, 0)
    mine[...] = xs[z]
    pl.semaphore_wait(barrier, (Q - 1) + (Z - 1) + (T - 1) + 1)
    for off in (4, 3, 5, 2, 6, 1, 7):
        x_z(off).start()
    for load in loads[1:4]:
        load.wait()
    cotangents(0)
    spread(0)
    cotangents(1)
    spread(1)
    first_hop(0)

    def produce(j, _):
        cotangents(j)
        spread(j)
        first_hop(j - 1)
        return 0

    lax.fori_loop(2, J, produce, 0)
    first_hop(J - 1)

    def x_a(off):
        part = xt.at[A, yhi, pl.ds(xrow, TOK), tokens(q)]
        return remote(part, part, xa_s.at[off], xa_r.at[off], x_peer(off))

    def y_b(off):
        part = xt.at[B, yhi, pl.ds(xrow, TOK), tokens(q)]
        return remote(part, part, yb_s.at[off], yb_r.at[off], y_peer(off))

    def y_a(off):
        part = xt.at[A, yhi, :, tokens(q)]
        return remote(part, part, ya_s.at[off], ya_r.at[off], y_peer(off))

    def x_b(off, lo):
        part = xt.at[B, :, pl.ds(xrow, TOK), tokens(lo * 2 + core)]
        return remote(part, part, xb_s.at[lo, off], xb_r.at[lo, off], x_peer(off))

    def y_far(way):
        src = lax.rem(yy + 4 - way, 4)
        hi, lo = lax.div(src, 2), lax.rem(src, 2)
        at = pl.ds(0 if way == 1 else 2, 2)
        part = xt.at[at, hi, :, tokens(lo * 2 + core)]
        return remote(part, part, ya_s.at[way - 1], ya_r.at[way - 1], y_peer(way))

    def x_far(way, lo):
        row = aligned(lax.rem(x + XN - way, XN) * TOK)
        at = pl.ds(4 if way == 1 else 6, 2)
        part = xt.at[at, :, pl.ds(row, TOK), tokens(lo * 2 + core)]
        return remote(part, part, xb_s.at[lo, way - 1], xb_r.at[lo, way - 1], x_peer(way))

    def swap_a(off):
        src = lax.rem(yy + off, 4)
        hi, lo = lax.div(src, 2), lax.rem(src, 2)
        part = xt.at[A, hi, :, tokens(lo * 2 + core)]
        return remote(part, part, ca_s.at[off], ca_r.at[off], core_peer)

    def swap_b(off, lo):
        row = aligned(lax.rem(x + off, XN) * TOK)
        part = xt.at[B, :, pl.ds(row, TOK), tokens(lo * 2 + core)]
        return remote(part, part, co_s.at[lo, off], co_r.at[lo, off], core_peer)

    for off in range(1, Z):
        x_z(off).wait_recv()
    for off in range(1, XN):
        x_a(off).start()
        y_b(off).start()

    cross = (((1,), (1,)), ((), ()))
    gram[...] = jnp.zeros_like(gram)
    loads[4].wait()

    def gram_x(k, _):
        part = x_v[:, pl.ds(aligned(k * 1024), 1024)]
        gram[0] += lax.dot_general(part, part, cross, preferred_element_type=f32)
        return 0

    lax.fori_loop(0, D // 1024, gram_x, 0)

    def gram_cot(k, _):
        at = pl.ds(aligned(k * 512), 512)
        gate = g_v[:, at].astype(f32)
        upper = (c_v[:, at].astype(f32) * (gate * jax.nn.sigmoid(gate))).astype(bf16)
        gate = gc[:, at]
        gram[1] += lax.dot_general(
            gate, gate, cross, preferred_element_type=f32
        ) + lax.dot_general(upper, upper, cross, preferred_element_type=f32)
        return 0

    lax.fori_loop(0, COLS // 512, gram_cot, 0)

    for e in range(TOK // SEQ):
        at = slice(e * SEQ, (e + 1) * SEQ)
        ghost = jnp.sum(gram[0, at, at] * gram[1, at, at], axis=1, keepdims=True)
        ghost = jnp.sum(ghost, axis=0, keepdims=True)
        rest = jnp.sum(other_v[e : e + 1, :], axis=1, keepdims=True)
        pn[0, e : e + 1, :] = jnp.broadcast_to(ghost + rest, (1, 128))
    pn[0, 2:8, :] = jnp.zeros((6, 128), f32)

    def norms(off):
        return remote(pn.at[0], pn.at[off], pn_s.at[off], pn_r.at[off], t_peer(off))

    for off in range(1, T):
        norms(off).start()

    def factor_q(off):
        return remote(fac.at[z, q], fac.at[z, q], fq_s.at[off], fq_r.at[off], q_peer(off))

    def factor_z(off):
        return remote(fac.at[z], fac.at[z], fz_s.at[off], fz_r.at[off], z_peer(off))

    def second_hop(j, _):
        next_hop(2, j)
        return 0

    for off in range(1, XN):
        y_b(off).wait_recv()
    for off in (1, 3):
        for lo in range(2):
            x_b(off, lo).start()
    lax.fori_loop(0, 1, second_hop, 0)

    for off in range(1, T):
        norms(off).wait_recv()
    total = jnp.zeros((8, 128), f32)
    for t in range(T):
        total = total + pn[lax.rem(tn + T - t, T)]
    fac[z, q] = clip_bound / jnp.maximum(jnp.sqrt(total), clip_bound)
    for off in range(1, Q):
        factor_q(off).start()

    for off in range(1, XN):
        x_a(off).wait_recv()
    for off in (1, 3):
        y_a(off).start()
    swap_a(0).start()
    for lo in range(2):
        swap_b(0, lo).start()
    lax.fori_loop(1, 4, second_hop, 0)

    for off in range(1, Q):
        factor_q(off).wait_recv()
    for off in range(1, Z):
        factor_z(off).start()

    lax.fori_loop(4, J, second_hop, 0)

    for off in (1, 3):
        y_a(off).wait_recv()
        y_far(off).start()
        for lo in range(2):
            x_b(off, lo).wait_recv()
            x_far(off, lo).start()
        swap_a(4 - off).start()
        for lo in range(2):
            swap_b(4 - off, lo).start()

    for off in range(1, Z):
        factor_z(off).wait_recv()

    def scale(j, src):
        at = pl.ds(aligned(j * W), W)
        for part in range(Q):
            for e in range(TOK // SEQ):
                block = cb[j, src, part, e * SEQ : (e + 1) * SEQ, :].astype(f32)
                block = block * fac[src, part, e : e + 1, :]
                cs[src, pl.ds(part * TOK + e * SEQ, SEQ), at] = block.astype(bf16)

    def scale_near(j, _):
        for off in (0, 1, Z - 1):
            scale(j, lax.rem(z + off, Z))
        return 0

    lax.fori_loop(0, J, scale_near, 0)

    def third_hop(j):
        next_hop(3, j)
        for off in (2, Z - 2):
            scale(j, lax.rem(z + off, Z))

    def third_hops(j, _):
        third_hop(j)
        return 0

    lax.fori_loop(0, AHEAD, third_hops, 0)

    for way in (1, 3):
        y_far(way).wait_recv()
        for lo in range(2):
            x_far(way, lo).wait_recv()
    swap_a(2).start()
    for lo in range(2):
        swap_b(2, lo).start()

    def place(j, part):
        return out_ref.at[:, pl.ds(aligned(part * PART + j * W), W)]

    def give(j, off):
        to = lax.rem(q + off, Q)
        return remote(
            ob.at[j, to], place(j, q), out_s.at[j, off], out_r.at[j, off], q_peer(off)
        )

    def keep(j):
        return pltpu.make_async_copy(ob.at[j, q], place(j, q), own_s.at[j])

    def product(half, j, offs):
        at = pl.ds(aligned(j * W), W)
        grad = acc[half, :, at]
        for off in offs:
            src = lax.rem(z + off, Z)
            grad += jnp.dot(xt[src, half], cs[src, :, at], preferred_element_type=f32)
        return grad

    def multiply_near(half, _):
        grad = jnp.dot(xt[z, half], cs[z], preferred_element_type=f32)
        for off in (1, Z - 1):
            src = lax.rem(z + off, Z)
            grad += jnp.dot(xt[src, half], cs[src], preferred_element_type=f32)
        acc[half] = grad
        return 0

    def multiply_early(j):
        for half in range(2):
            acc[half, :, pl.ds(aligned(j * W), W)] = product(half, j, (2, Z - 2, 3, Z - 3))

    def multiply_late(j):
        hop_plus(4, j).wait_recv()
        hop_minus(4, j).wait_recv()
        scale(j, lax.rem(z + 4, Z))
        for half in range(2):
            grad = product(half, j, (4,)).astype(bf16)
            ob[j, 2 * half] = grad[:OWN]
            ob[j, 2 * half + 1] = grad[OWN:]
        for off in range(1, Q):
            give(j, off).start()
        keep(j).start()

    for off in range(Q):
        swap_a(off).wait_recv()
        for lo in range(2):
            swap_b(off, lo).wait_recv()
    lax.fori_loop(0, 2, multiply_near, 0)

    def last_hops(i, _):
        @pl.when((i + LAG >= AHEAD) & (i + LAG < J))
        def _():
            third_hop(i + LAG)

        @pl.when(i < J)
        def _():
            next_hop(4, i)
            for off in (3, Z - 3):
                scale(i, lax.rem(z + off, Z))

        @pl.when(i > 0)
        def _():
            multiply_late(i - 1)

        @pl.when(i < J)
        def _():
            multiply_early(i)

        return 0

    lax.fori_loop(0, J + 1, last_hops, 0)

    for off in range(1, Z):
        x_z(off).wait_send()
        factor_z(off).wait_send()
    for off in range(1, T):
        norms(off).wait_send()
    for off in range(1, Q):
        x_a(off).wait_send()
        y_b(off).wait_send()
        factor_q(off).wait_send()
    for off in (1, 3):
        y_a(off).wait_send()
        y_far(off).wait_send()
        for lo in range(2):
            x_b(off, lo).wait_send()
            x_far(off, lo).wait_send()
    for off in range(Q):
        swap_a(off).wait_send()
        for lo in range(2):
            swap_b(off, lo).wait_send()

    def finish(j, _):
        for off in range(1, Q):
            quad(j, off).wait_send()
        for h in range(1, 5):
            hop_plus(h, j).wait_send()
            hop_minus(h, j).wait_send()
        for off in range(1, Q):
            give(j, off).wait_send()
            give(j, off).wait_recv()
        keep(j).wait()
        return 0

    lax.fori_loop(0, J, finish, 0)


def shards(layer_input, gate_pre, up_pre, hidden_cot, other_norms, noise_gate):
    dma = pltpu.SemaphoreType.DMA
    anywhere = pl.BlockSpec(memory_space=pl.ANY)
    grad = pl.pallas_call(
        kernel,
        out_shape=jax.ShapeDtypeStruct((OWN, COLS), bf16),
        in_specs=[anywhere] * 5,
        out_specs=anywhere,
        scratch_shapes=[
            pltpu.VMEM((TOK, D), bf16),
            pltpu.VMEM((TOK, COLS), bf16),
            pltpu.VMEM((TOK, COLS), bf16),
            pltpu.VMEM((TOK, COLS), bf16),
            pltpu.VMEM((2, 16), f32),
            pltpu.VMEM((TOK, COLS), bf16),
            pltpu.VMEM((J, Z, Q, TOK, W), bf16),
            pltpu.VMEM((Z, Q * TOK, PART), bf16),
            pltpu.VMEM((Z, 2, ROWS // 2, Q * TOK), bf16),
            pltpu.VMEM((Z, TOK, TOK), bf16),
            pltpu.VMEM((J, Q, OWN, W), bf16),
            pltpu.VMEM((2, ROWS // 2, PART), f32),
            pltpu.VMEM((2, TOK, TOK), f32),
            pltpu.VMEM((T, 8, 128), f32),
            pltpu.VMEM((Z, Q, 8, 128), f32),
            dma((5,)),
            dma((Z,)), dma((Z,)),
            dma((4,)), dma((4,)), dma((4,)), dma((4,)), dma((4,)), dma((4,)),
            dma((2, 4)), dma((2, 4)), dma((4,)), dma((4,)), dma((2, 4)), dma((2, 4)),
            dma((J, Q)), dma((J, Q)),
            dma((4, J)), dma((4, J)), dma((4, J)), dma((4, J)),
            dma((T,)), dma((T,)), dma((Q,)), dma((Q,)), dma((Z,)), dma((Z,)),
            dma((J, Q)), dma((J, Q)), dma((J,)),
        ],
        compiler_params=pltpu.CompilerParams(
            collective_id=0, has_side_effects=True, vmem_limit_bytes=40 * 1024 * 1024
        ),
        cost_estimate=pl.CostEstimate(
            flops=2 * 4096 * 256 * 3584, bytes_accessed=8 * 1024 * 1024, transcendentals=128 * 3584
        ),
        name="clipped_gradient",
    )(*(pltpu.with_memory_space_constraint(a, pltpu.HBM) for a in (layer_input, gate_pre, up_pre, hidden_cot, other_norms)))
    return grad.astype(f32) + noise_gate.astype(f32)


def solution(mesh):
    placed = (
        P("dp", None),
        P("dp", "tensor"),
        P("dp", "tensor"),
        P("dp", "tensor"),
        P("dp", "tensor"),
        P("dp", "tensor"),
    )
    return jax.shard_map(
        shards, mesh=mesh, in_specs=placed, out_specs=P("dp", "tensor"), check_vma=False
    )
```

```python
import math

import jax
import jax.numpy as jnp
from jax import lax
from jax.experimental import pallas as pl
from jax.experimental.pallas import tpu as pltpu
from jax.sharding import PartitionSpec as P

D = 8192
FF = 28672
SEQ = 64
clip_ratio = 0.045
clip_bound = clip_ratio * math.sqrt(SEQ * D * FF)

Z = 8
Q = 4
XN = 4
T = 8
TOK = 128
COLS = 3584
PART = COLS // Q
W = 128
J = PART // W
ROWS = 1024
OWN = ROWS // Q
A, B = pl.ds(0, Z // 2), pl.ds(Z // 2, Z // 2)
AHEAD = 2
MESH = pl.DeviceIdType.MESH
f32 = jnp.float32
bf16 = jnp.bfloat16


def aligned(value, to=128):
    return pl.multiple_of(value, to)


def tokens(q):
    return pl.ds(aligned(q * TOK), TOK)


def kernel(
    x_hbm, g_hbm, u_hbm, c_hbm, other_hbm, out_ref,
    x_v, g_v, u_v, c_v, other_v, gc, cb, cs, xt, xc, xs, ob, acc, gram, pn, fac,
    in_sem, slice_sem, xz_s, xz_r, xa_s, xa_r, yb_s, yb_r, ya_s, ya_r, xb_s, xb_r, ca_s, ca_r, co_s, co_r,
    qa_s, qa_r, rp_s, rp_r, rm_s, rm_r, pn_s, pn_r, fq_s, fq_r, fz_s, fz_r, out_s, out_r, own_s,
):
    dp = lax.axis_index("dp")
    tn = lax.axis_index("tensor")
    z, q = lax.div(dp, Q), lax.rem(dp, Q)
    ylo, core = lax.div(q, 2), lax.rem(q, 2)
    x, yhi = lax.div(tn, 2), lax.rem(tn, 2)
    yy = yhi * 2 + ylo
    xrow = aligned(x * TOK)

    def zq(zd, qd):
        return (zd * Q + qd, tn)

    def x_peer(off):
        return (dp, lax.rem(x + off, XN) * 2 + yhi)

    def y_peer(off):
        to = lax.rem(yy + off, 4)
        return (z * Q + lax.rem(to, 2) * 2 + core, x * 2 + lax.div(to, 2))

    def z_peer(off):
        return zq(lax.rem(z + off, Z), q)

    def q_peer(off):
        return zq(z, lax.rem(q + off, Q))

    def t_peer(off):
        return (dp, lax.rem(tn + off, T))

    core_peer = zq(z, ylo * 2 + 1 - core)

    def remote(src, dst, send, recv, device):
        return pltpu.make_async_remote_copy(
            src_ref=src, dst_ref=dst, send_sem=send, recv_sem=recv,
            device_id=device, device_id_type=MESH,
        )

    loads = [
        pltpu.make_async_copy(src, dst, in_sem.at[i])
        for i, (src, dst) in enumerate(
            ((g_hbm, g_v), (u_hbm, u_v), (c_hbm, c_v), (x_hbm, x_v), (other_hbm, other_v))
        )
    ]

    def slice_of(zd):
        at = pl.ds(aligned(zd * ROWS + yhi * (ROWS // 2) + x * TOK), TOK)
        return pltpu.make_async_copy(x_hbm.at[:, at], xc.at[zd], slice_sem.at[zd])

    for zd in range(Z):
        slice_of(zd).start()
    for load in loads:
        load.start()

    barrier = pltpu.get_barrier_semaphore()

    def greet(device):
        pl.semaphore_signal(barrier, inc=1, device_id=device, device_id_type=MESH)

    for off in range(1, Q):
        greet(q_peer(off))
    for off in range(1, Z):
        greet(z_peer(off))
    for off in range(1, T):
        greet(t_peer(off))
    greet((z * Q + (1 - ylo) * 2 + core, x * 2 + 1 - yhi))

    def quad(j, off):
        to = lax.rem(q + off, Q)
        return remote(
            gc.at[:, pl.ds(aligned(to * PART + j * W), W)], cb.at[j, z, q],
            qa_s.at[j, off], qa_r.at[j, off], q_peer(off),
        )

    def cotangents(j):
        for part in range(Q):
            at = pl.ds(aligned(part * PART + j * W), W)
            gate = g_v[:, at].astype(f32)
            upper = u_v[:, at].astype(f32)
            cotan = c_v[:, at].astype(f32)
            sig = jax.nn.sigmoid(gate)
            slope = sig * (1.0 + gate * (1.0 - sig))
            gc[:, at] = (cotan * upper * slope).astype(bf16)

    def spread(j):
        for off in range(1, Q):
            quad(j, off).start()
        cb[j, z, q] = gc[:, pl.ds(aligned(q * PART + j * W), W)]

    def hop_plus(h, j):
        src = lax.rem(z + Z - {1: 0, 2: 1, 3: 2, 4: 3, 5: 2}[h], Z)
        block = cb.at[j, src]
        if h > 2:
            block = cb.at[j, src, pl.ds(2 if h == 5 else 0, 2)]
        return remote(block, block, rp_s.at[h - 1, j], rp_r.at[h - 1, j], z_peer(1))

    def hop_minus(h, j):
        src = lax.rem(z + {1: 0, 2: 1, 3: 2, 4: 3, 5: 2}[h], Z)
        block = cb.at[j, src]
        if h > 2:
            block = cb.at[j, src, pl.ds(0 if h == 5 else 2, 2)]
        return remote(block, block, rm_s.at[h - 1, j], rm_r.at[h - 1, j], z_peer(Z - 1))

    def first_hop(j):
        for off in range(1, Q):
            quad(j, off).wait_recv()
        hop_plus(1, j).start()
        hop_minus(1, j).start()

    def next_hop(h, j):
        hop_plus(h - 1, j).wait_recv()
        hop_plus(h, j).start()
        hop_minus(h - 1, j).wait_recv()
        hop_minus(h, j).start()

    def turn(zd, _):
        xs[zd] = xc[zd].T
        return 0

    mine = xt.at[z, yhi, pl.ds(xrow, TOK), tokens(q)]

    def x_z(off):
        return remote(xs.at[lax.rem(z + off, Z)], mine, xz_s.at[off], xz_r.at[off], z_peer(off))

    for zd in range(Z):
        slice_of(zd).wait()
    lax.fori_loop(0, Z, turn, 0)
    mine[...] = xs[z]
    pl.semaphore_wait(barrier, (Q - 1) + (Z - 1) + (T - 1) + 1)
    for off in (4, 3, 5, 2, 6, 1, 7):
        x_z(off).start()
    for load in loads[:3]:
        load.wait()
    cotangents(0)
    spread(0)
    cotangents(1)
    spread(1)
    first_hop(0)

    def produce(j, _):
        cotangents(j)
        spread(j)
        first_hop(j - 1)
        return 0

    lax.fori_loop(2, J, produce, 0)
    first_hop(J - 1)

    def x_a(off):
        part = xt.at[A, yhi, pl.ds(xrow, TOK), tokens(q)]
        return remote(part, part, xa_s.at[off], xa_r.at[off], x_peer(off))

    def y_b(off):
        part = xt.at[B, yhi, pl.ds(xrow, TOK), tokens(q)]
        return remote(part, part, yb_s.at[off], yb_r.at[off], y_peer(off))

    def y_a(off):
        part = xt.at[A, yhi, :, tokens(q)]
        return remote(part, part, ya_s.at[off], ya_r.at[off], y_peer(off))

    def x_b(off, lo):
        part = xt.at[B, :, pl.ds(xrow, TOK), tokens(lo * 2 + core)]
        return remote(part, part, xb_s.at[lo, off], xb_r.at[lo, off], x_peer(off))

    def y_far(way):
        src = lax.rem(yy + 4 - way, 4)
        hi, lo = lax.div(src, 2), lax.rem(src, 2)
        at = pl.ds(0 if way == 1 else 2, 2)
        part = xt.at[at, hi, :, tokens(lo * 2 + core)]
        return remote(part, part, ya_s.at[way - 1], ya_r.at[way - 1], y_peer(way))

    def x_far(way, lo):
        row = aligned(lax.rem(x + XN - way, XN) * TOK)
        at = pl.ds(4 if way == 1 else 6, 2)
        part = xt.at[at, :, pl.ds(row, TOK), tokens(lo * 2 + core)]
        return remote(part, part, xb_s.at[lo, way - 1], xb_r.at[lo, way - 1], x_peer(way))

    def swap_a(off):
        src = lax.rem(yy + off, 4)
        hi, lo = lax.div(src, 2), lax.rem(src, 2)
        part = xt.at[A, hi, :, tokens(lo * 2 + core)]
        return remote(part, part, ca_s.at[off], ca_r.at[off], core_peer)

    def swap_b(off, lo):
        row = aligned(lax.rem(x + off, XN) * TOK)
        part = xt.at[B, :, pl.ds(row, TOK), tokens(lo * 2 + core)]
        return remote(part, part, co_s.at[lo, off], co_r.at[lo, off], core_peer)

    for off in range(1, Z):
        x_z(off).wait_recv()
    for off in range(1, XN):
        x_a(off).start()
        y_b(off).start()

    cross = (((1,), (1,)), ((), ()))
    gram[...] = jnp.zeros_like(gram)
    loads[3].wait()
    loads[4].wait()

    def gram_x(k, _):
        part = x_v[:, pl.ds(aligned(k * 1024), 1024)]
        gram[0] += lax.dot_general(part, part, cross, preferred_element_type=f32)
        return 0

    lax.fori_loop(0, D // 1024, gram_x, 0)

    def gram_cot(k, _):
        at = pl.ds(aligned(k * 512), 512)
        gate = g_v[:, at].astype(f32)
        upper = (c_v[:, at].astype(f32) * (gate * jax.nn.sigmoid(gate))).astype(bf16)
        gate = gc[:, at]
        gram[1] += lax.dot_general(
            gate, gate, cross, preferred_element_type=f32
        ) + lax.dot_general(upper, upper, cross, preferred_element_type=f32)
        return 0

    lax.fori_loop(0, COLS // 512, gram_cot, 0)

    for e in range(TOK // SEQ):
        at = slice(e * SEQ, (e + 1) * SEQ)
        ghost = jnp.sum(gram[0, at, at] * gram[1, at, at], axis=1, keepdims=True)
        ghost = jnp.sum(ghost, axis=0, keepdims=True)
        rest = jnp.sum(other_v[e : e + 1, :], axis=1, keepdims=True)
        pn[0, e : e + 1, :] = jnp.broadcast_to(ghost + rest, (1, 128))
    pn[0, 2:8, :] = jnp.zeros((6, 128), f32)

    def norms(off):
        return remote(pn.at[0], pn.at[off], pn_s.at[off], pn_r.at[off], t_peer(off))

    for off in range(1, T):
        norms(off).start()

    def factor_q(off):
        return remote(fac.at[z, q], fac.at[z, q], fq_s.at[off], fq_r.at[off], q_peer(off))

    def factor_z(off):
        return remote(fac.at[z], fac.at[z], fz_s.at[off], fz_r.at[off], z_peer(off))

    def second_hop(j, _):
        next_hop(2, j)
        return 0

    for off in range(1, XN):
        y_b(off).wait_recv()
    for off in (1, 3):
        for lo in range(2):
            x_b(off, lo).start()
    lax.fori_loop(0, 1, second_hop, 0)

    for off in range(1, T):
        norms(off).wait_recv()
    total = jnp.zeros((8, 128), f32)
    for t in range(T):
        total = total + pn[lax.rem(tn + T - t, T)]
    fac[z, q] = clip_bound / jnp.maximum(jnp.sqrt(total), clip_bound)
    for off in range(1, Q):
        factor_q(off).start()

    for off in range(1, XN):
        x_a(off).wait_recv()
    for off in (1, 3):
        y_a(off).start()
    swap_a(0).start()
    for lo in range(2):
        swap_b(0, lo).start()
    lax.fori_loop(1, 4, second_hop, 0)

    for off in range(1, Q):
        factor_q(off).wait_recv()
    for off in range(1, Z):
        factor_z(off).start()

    lax.fori_loop(4, J, second_hop, 0)

    for off in (1, 3):
        y_a(off).wait_recv()
        y_far(off).start()
        for lo in range(2):
            x_b(off, lo).wait_recv()
            x_far(off, lo).start()
        swap_a(4 - off).start()
        for lo in range(2):
            swap_b(4 - off, lo).start()

    for off in range(1, Z):
        factor_z(off).wait_recv()

    def scale(j, src):
        at = pl.ds(aligned(j * W), W)
        for part in range(Q):
            for e in range(TOK // SEQ):
                block = cb[j, src, part, e * SEQ : (e + 1) * SEQ, :].astype(f32)
                block = block * fac[src, part, e : e + 1, :]
                cs[src, pl.ds(part * TOK + e * SEQ, SEQ), at] = block.astype(bf16)

    def scale_near(j, _):
        for off in (0, 1, Z - 1):
            scale(j, lax.rem(z + off, Z))
        return 0

    lax.fori_loop(0, J, scale_near, 0)

    def third_hop(j):
        next_hop(3, j)
        rest_of_third(j)

    def rest_of_third(j):
        hop_plus(5, j).start()
        hop_minus(5, j).start()
        for off in (2, Z - 2):
            scale(j, lax.rem(z + off, Z))

    def third_hops(j, _):
        third_hop(j)
        return 0

    lax.fori_loop(0, AHEAD, third_hops, 0)

    for way in (1, 3):
        y_far(way).wait_recv()
        for lo in range(2):
            x_far(way, lo).wait_recv()
    swap_a(2).start()
    for lo in range(2):
        swap_b(2, lo).start()

    def place(j, part):
        return out_ref.at[:, pl.ds(aligned(part * PART + j * W), W)]

    def give(j, off):
        to = lax.rem(q + off, Q)
        return remote(
            ob.at[j, to], place(j, q), out_s.at[j, off], out_r.at[j, off], q_peer(off)
        )

    def keep(j):
        return pltpu.make_async_copy(ob.at[j, q], place(j, q), own_s.at[j])

    def product(half, j, offs):
        at = pl.ds(aligned(j * W), W)
        grad = acc[half, :, at]
        for off in offs:
            src = lax.rem(z + off, Z)
            grad += jnp.dot(xt[src, half], cs[src, :, at], preferred_element_type=f32)
        return grad

    def multiply_near(half, _):
        grad = jnp.dot(xt[z, half], cs[z], preferred_element_type=f32)
        for off in (1, Z - 1):
            src = lax.rem(z + off, Z)
            grad += jnp.dot(xt[src, half], cs[src], preferred_element_type=f32)
        acc[half] = grad
        return 0

    def multiply_early(j):
        for half in range(2):
            acc[half, :, pl.ds(aligned(j * W), W)] = product(half, j, (2, Z - 2, 3, Z - 3))

    def multiply_late(j):
        hop_plus(4, j).wait_recv()
        hop_minus(4, j).wait_recv()
        scale(j, lax.rem(z + 4, Z))
        for half in range(2):
            grad = product(half, j, (4,)).astype(bf16)
            ob[j, 2 * half] = grad[:OWN]
            ob[j, 2 * half + 1] = grad[OWN:]
        for off in range(1, Q):
            give(j, off).start()
        keep(j).start()

    for off in range(Q):
        swap_a(off).wait_recv()
        for lo in range(2):
            swap_b(off, lo).wait_recv()
    lax.fori_loop(0, 2, multiply_near, 0)

    def last_hops(i, _):
        more = (i >= AHEAD) & (i < J)

        @pl.when(more)
        def _():
            next_hop(3, i)

        @pl.when(i <= J)
        def _():
            next_hop(4, i - 1)

        @pl.when(more)
        def _():
            rest_of_third(i)

        @pl.when(i > 1)
        def _():
            multiply_late(i - 2)

        @pl.when(i <= J)
        def _():
            hop_plus(5, i - 1).wait_recv()
            hop_minus(5, i - 1).wait_recv()
            for off in (3, Z - 3):
                scale(i - 1, lax.rem(z + off, Z))
            multiply_early(i - 1)

        return 0

    lax.fori_loop(1, J + 2, last_hops, 0)

    for off in range(1, Z):
        x_z(off).wait_send()
        factor_z(off).wait_send()
    for off in range(1, T):
        norms(off).wait_send()
    for off in range(1, Q):
        x_a(off).wait_send()
        y_b(off).wait_send()
        factor_q(off).wait_send()
    for off in (1, 3):
        y_a(off).wait_send()
        y_far(off).wait_send()
        for lo in range(2):
            x_b(off, lo).wait_send()
            x_far(off, lo).wait_send()
    for off in range(Q):
        swap_a(off).wait_send()
        for lo in range(2):
            swap_b(off, lo).wait_send()

    def finish(j, _):
        for off in range(1, Q):
            quad(j, off).wait_send()
        for h in range(1, 6):
            hop_plus(h, j).wait_send()
            hop_minus(h, j).wait_send()
        for off in range(1, Q):
            give(j, off).wait_send()
            give(j, off).wait_recv()
        keep(j).wait()
        return 0

    lax.fori_loop(0, J, finish, 0)


def shards(layer_input, gate_pre, up_pre, hidden_cot, other_norms, noise_gate):
    dma = pltpu.SemaphoreType.DMA
    anywhere = pl.BlockSpec(memory_space=pl.ANY)
    grad = pl.pallas_call(
        kernel,
        out_shape=jax.ShapeDtypeStruct((OWN, COLS), bf16),
        in_specs=[anywhere] * 5,
        out_specs=anywhere,
        scratch_shapes=[
            pltpu.VMEM((TOK, D), bf16),
            pltpu.VMEM((TOK, COLS), bf16),
            pltpu.VMEM((TOK, COLS), bf16),
            pltpu.VMEM((TOK, COLS), bf16),
            pltpu.VMEM((2, 16), f32),
            pltpu.VMEM((TOK, COLS), bf16),
            pltpu.VMEM((J, Z, Q, TOK, W), bf16),
            pltpu.VMEM((Z, Q * TOK, PART), bf16),
            pltpu.VMEM((Z, 2, ROWS // 2, Q * TOK), bf16),
            pltpu.VMEM((Z, TOK, TOK), bf16),
            pltpu.VMEM((Z, TOK, TOK), bf16),
            pltpu.VMEM((J, Q, OWN, W), bf16),
            pltpu.VMEM((2, ROWS // 2, PART), f32),
            pltpu.VMEM((2, TOK, TOK), f32),
            pltpu.VMEM((T, 8, 128), f32),
            pltpu.VMEM((Z, Q, 8, 128), f32),
            dma((5,)), dma((Z,)),
            dma((Z,)), dma((Z,)),
            dma((4,)), dma((4,)), dma((4,)), dma((4,)), dma((4,)), dma((4,)),
            dma((2, 4)), dma((2, 4)), dma((4,)), dma((4,)), dma((2, 4)), dma((2, 4)),
            dma((J, Q)), dma((J, Q)),
            dma((5, J)), dma((5, J)), dma((5, J)), dma((5, J)),
            dma((T,)), dma((T,)), dma((Q,)), dma((Q,)), dma((Z,)), dma((Z,)),
            dma((J, Q)), dma((J, Q)), dma((J,)),
        ],
        compiler_params=pltpu.CompilerParams(
            collective_id=0, has_side_effects=True, vmem_limit_bytes=40 * 1024 * 1024
        ),
        cost_estimate=pl.CostEstimate(
            flops=2 * 4096 * 256 * 3584, bytes_accessed=8 * 1024 * 1024, transcendentals=128 * 3584
        ),
        name="clipped_gradient",
    )(*(pltpu.with_memory_space_constraint(a, pltpu.HBM) for a in (layer_input, gate_pre, up_pre, hidden_cot, other_norms)))
    return grad.astype(f32) + noise_gate.astype(f32)


def solution(mesh):
    placed = (
        P("dp", None),
        P("dp", "tensor"),
        P("dp", "tensor"),
        P("dp", "tensor"),
        P("dp", "tensor"),
        P("dp", "tensor"),
    )
    return jax.shard_map(
        shards, mesh=mesh, in_specs=placed, out_specs=P("dp", "tensor"), check_vma=False
    )
```

```python
import math

import jax
import jax.numpy as jnp
from jax import lax
from jax.experimental import pallas as pl
from jax.experimental.pallas import tpu as pltpu
from jax.sharding import PartitionSpec as P

D = 8192
FF = 28672
SEQ = 64
clip_ratio = 0.045
clip_bound = clip_ratio * math.sqrt(SEQ * D * FF)

Z = 8
Q = 4
XN = 4
T = 8
TOK = 128
COLS = 3584
PART = COLS // Q
W = 128
J = PART // W
ROWS = 1024
OWN = ROWS // Q
A, B = pl.ds(0, Z // 2), pl.ds(Z // 2, Z // 2)
AHEAD = 2
MESH = pl.DeviceIdType.MESH
f32 = jnp.float32
bf16 = jnp.bfloat16


def aligned(value, to=128):
    return pl.multiple_of(value, to)


def tokens(q):
    return pl.ds(aligned(q * TOK), TOK)


def kernel(
    x_hbm, g_hbm, u_hbm, c_hbm, other_hbm, out_ref,
    x_v, g_v, u_v, c_v, other_v, gc, cb, cs, xt, xc, xs, ob, acc, gram, pn, fq, fac,
    in_sem, slice_sem, xz_s, xz_r, xa_s, xa_r, yb_s, yb_r, ya_s, ya_r, xb_s, xb_r, ca_s, ca_r, co_s, co_r,
    qa_s, qa_r, rp_s, rp_r, rm_s, rm_r, pn_s, pn_r, fq_s, fq_r, fz_s, fz_r, out_s, out_r, own_s,
):
    dp = lax.axis_index("dp")
    tn = lax.axis_index("tensor")
    z, q = lax.div(dp, Q), lax.rem(dp, Q)
    ylo, core = lax.div(q, 2), lax.rem(q, 2)
    x, yhi = lax.div(tn, 2), lax.rem(tn, 2)
    yy = yhi * 2 + ylo
    xrow = aligned(x * TOK)

    def zq(zd, qd):
        return (zd * Q + qd, tn)

    def x_peer(off):
        return (dp, lax.rem(x + off, XN) * 2 + yhi)

    def y_peer(off):
        to = lax.rem(yy + off, 4)
        return (z * Q + lax.rem(to, 2) * 2 + core, x * 2 + lax.div(to, 2))

    def z_peer(off):
        return zq(lax.rem(z + off, Z), q)

    def q_peer(off):
        return zq(z, lax.rem(q + off, Q))

    def t_peer(off):
        return (dp, lax.rem(tn + off, T))

    core_peer = zq(z, ylo * 2 + 1 - core)

    def remote(src, dst, send, recv, device):
        return pltpu.make_async_remote_copy(
            src_ref=src, dst_ref=dst, send_sem=send, recv_sem=recv,
            device_id=device, device_id_type=MESH,
        )

    loads = [
        pltpu.make_async_copy(src, dst, in_sem.at[i])
        for i, (src, dst) in enumerate(
            ((g_hbm, g_v), (u_hbm, u_v), (c_hbm, c_v), (x_hbm, x_v), (other_hbm, other_v))
        )
    ]

    def slice_of(zd):
        at = pl.ds(aligned(zd * ROWS + yhi * (ROWS // 2) + x * TOK), TOK)
        return pltpu.make_async_copy(x_hbm.at[:, at], xc.at[zd], slice_sem.at[zd])

    for zd in range(Z):
        slice_of(zd).start()
    for load in loads:
        load.start()

    barrier = pltpu.get_barrier_semaphore()

    def greet(device):
        pl.semaphore_signal(barrier, inc=1, device_id=device, device_id_type=MESH)

    for off in range(1, Q):
        greet(q_peer(off))
    for off in range(1, Z):
        greet(z_peer(off))
    for off in range(1, T):
        greet(t_peer(off))
    greet((z * Q + (1 - ylo) * 2 + core, x * 2 + 1 - yhi))

    def quad(j, off):
        to = lax.rem(q + off, Q)
        return remote(
            gc.at[:, pl.ds(aligned(to * PART + j * W), W)], cb.at[j, z, q],
            qa_s.at[j, off], qa_r.at[j, off], q_peer(off),
        )

    def cotangents(j):
        for part in range(Q):
            at = pl.ds(aligned(part * PART + j * W), W)
            gate = g_v[:, at].astype(f32)
            upper = u_v[:, at].astype(f32)
            cotan = c_v[:, at].astype(f32)
            sig = jax.nn.sigmoid(gate)
            slope = sig * (1.0 + gate * (1.0 - sig))
            gc[:, at] = (cotan * upper * slope).astype(bf16)

    def spread(j):
        for off in range(1, Q):
            quad(j, off).start()
        cb[j, z, q] = gc[:, pl.ds(aligned(q * PART + j * W), W)]

    def hop_plus(h, j):
        src = lax.rem(z + Z - {1: 0, 2: 1, 3: 2, 4: 3, 5: 2}[h], Z)
        block = cb.at[j, src]
        if h > 2:
            block = cb.at[j, src, pl.ds(2 if h == 5 else 0, 2)]
        return remote(block, block, rp_s.at[h - 1, j], rp_r.at[h - 1, j], z_peer(1))

    def hop_minus(h, j):
        src = lax.rem(z + {1: 0, 2: 1, 3: 2, 4: 3, 5: 2}[h], Z)
        block = cb.at[j, src]
        if h > 2:
            block = cb.at[j, src, pl.ds(0 if h == 5 else 2, 2)]
        return remote(block, block, rm_s.at[h - 1, j], rm_r.at[h - 1, j], z_peer(Z - 1))

    def first_hop(j):
        for off in range(1, Q):
            quad(j, off).wait_recv()
        hop_plus(1, j).start()
        hop_minus(1, j).start()

    def next_hop(h, j):
        hop_plus(h - 1, j).wait_recv()
        hop_plus(h, j).start()
        hop_minus(h - 1, j).wait_recv()
        hop_minus(h, j).start()

    def turn(zd, _):
        xs[zd] = xc[zd].T
        return 0

    mine = xt.at[z, yhi, pl.ds(xrow, TOK), tokens(q)]

    def x_z(off):
        return remote(xs.at[lax.rem(z + off, Z)], mine, xz_s.at[off], xz_r.at[off], z_peer(off))

    for zd in range(Z):
        slice_of(zd).wait()
    lax.fori_loop(0, Z, turn, 0)
    mine[...] = xs[z]
    pl.semaphore_wait(barrier, (Q - 1) + (Z - 1) + (T - 1) + 1)
    for off in (4, 3, 5, 2, 6, 1, 7):
        x_z(off).start()
    for load in loads[:3]:
        load.wait()
    cotangents(0)
    spread(0)
    cotangents(1)
    spread(1)
    first_hop(0)

    def produce(j, _):
        cotangents(j)
        spread(j)
        first_hop(j - 1)
        return 0

    lax.fori_loop(2, J, produce, 0)
    first_hop(J - 1)

    def x_a(off):
        part = xt.at[A, yhi, pl.ds(xrow, TOK), tokens(q)]
        return remote(part, part, xa_s.at[off], xa_r.at[off], x_peer(off))

    def y_b(off):
        part = xt.at[B, yhi, pl.ds(xrow, TOK), tokens(q)]
        return remote(part, part, yb_s.at[off], yb_r.at[off], y_peer(off))

    def y_a(off):
        part = xt.at[A, yhi, :, tokens(q)]
        return remote(part, part, ya_s.at[off], ya_r.at[off], y_peer(off))

    def x_b(off, lo):
        part = xt.at[B, :, pl.ds(xrow, TOK), tokens(lo * 2 + core)]
        return remote(part, part, xb_s.at[lo, off], xb_r.at[lo, off], x_peer(off))

    def y_far(way):
        src = lax.rem(yy + 4 - way, 4)
        hi, lo = lax.div(src, 2), lax.rem(src, 2)
        at = pl.ds(0 if way == 1 else 2, 2)
        part = xt.at[at, hi, :, tokens(lo * 2 + core)]
        return remote(part, part, ya_s.at[way - 1], ya_r.at[way - 1], y_peer(way))

    def x_far(way, lo):
        row = aligned(lax.rem(x + XN - way, XN) * TOK)
        at = pl.ds(4 if way == 1 else 6, 2)
        part = xt.at[at, :, pl.ds(row, TOK), tokens(lo * 2 + core)]
        return remote(part, part, xb_s.at[lo, way - 1], xb_r.at[lo, way - 1], x_peer(way))

    def swap_a(off):
        src = lax.rem(yy + off, 4)
        hi, lo = lax.div(src, 2), lax.rem(src, 2)
        part = xt.at[A, hi, :, tokens(lo * 2 + core)]
        return remote(part, part, ca_s.at[off], ca_r.at[off], core_peer)

    def swap_b(off, lo):
        row = aligned(lax.rem(x + off, XN) * TOK)
        part = xt.at[B, :, pl.ds(row, TOK), tokens(lo * 2 + core)]
        return remote(part, part, co_s.at[lo, off], co_r.at[lo, off], core_peer)

    for off in range(1, Z):
        x_z(off).wait_recv()
    for off in range(1, XN):
        x_a(off).start()
        y_b(off).start()

    cross = (((1,), (1,)), ((), ()))
    gram[...] = jnp.zeros_like(gram)
    loads[3].wait()
    loads[4].wait()

    def gram_x(k, _):
        part = x_v[:, pl.ds(aligned(k * 1024), 1024)]
        gram[0] += lax.dot_general(part, part, cross, preferred_element_type=f32)
        return 0

    lax.fori_loop(0, D // 1024, gram_x, 0)

    def gram_cot(k, _):
        at = pl.ds(aligned(k * 512), 512)
        gate = g_v[:, at].astype(f32)
        upper = (c_v[:, at].astype(f32) * (gate * jax.nn.sigmoid(gate))).astype(bf16)
        gate = gc[:, at]
        gram[1] += lax.dot_general(
            gate, gate, cross, preferred_element_type=f32
        ) + lax.dot_general(upper, upper, cross, preferred_element_type=f32)
        return 0

    lax.fori_loop(0, COLS // 512, gram_cot, 0)

    for e in range(TOK // SEQ):
        at = slice(e * SEQ, (e + 1) * SEQ)
        ghost = jnp.sum(gram[0, at, at] * gram[1, at, at], axis=1, keepdims=True)
        ghost = jnp.sum(ghost, axis=0, keepdims=True)
        rest = jnp.sum(other_v[e : e + 1, :], axis=1, keepdims=True)
        pn[0, e : e + 1, :] = jnp.broadcast_to(ghost + rest, (1, 128))
    pn[0, 2:8, :] = jnp.zeros((6, 128), f32)

    def norms(off):
        return remote(pn.at[0], pn.at[off], pn_s.at[off], pn_r.at[off], t_peer(off))

    for off in range(1, T):
        norms(off).start()

    def factor_q(off):
        return remote(fq.at[q], fq.at[q], fq_s.at[off], fq_r.at[off], q_peer(off))

    def factor_z(off):
        return remote(fac.at[z], fac.at[z], fz_s.at[off], fz_r.at[off], z_peer(off))

    def second_hop(j, _):
        next_hop(2, j)
        return 0

    for off in range(1, XN):
        y_b(off).wait_recv()
    for off in (1, 3):
        for lo in range(2):
            x_b(off, lo).start()
    lax.fori_loop(0, 1, second_hop, 0)

    for off in range(1, T):
        norms(off).wait_recv()
    total = jnp.zeros((8, 128), f32)
    for t in range(T):
        total = total + pn[lax.rem(tn + T - t, T)]
    fq[q] = clip_bound / jnp.maximum(jnp.sqrt(total), clip_bound)
    for off in range(1, Q):
        factor_q(off).start()

    for off in range(1, XN):
        x_a(off).wait_recv()
    for off in (1, 3):
        y_a(off).start()
    swap_a(0).start()
    for lo in range(2):
        swap_b(0, lo).start()
    lax.fori_loop(1, 4, second_hop, 0)

    for off in range(1, Q):
        factor_q(off).wait_recv()
    for part in range(Q):
        fac[z, 2 * part : 2 * part + 2, :] = fq[part, 0:2, :]
    for off in range(1, Z):
        factor_z(off).start()

    lax.fori_loop(4, J, second_hop, 0)

    for off in (1, 3):
        y_a(off).wait_recv()
        y_far(off).start()
        for lo in range(2):
            x_b(off, lo).wait_recv()
            x_far(off, lo).start()
        swap_a(4 - off).start()
        for lo in range(2):
            swap_b(4 - off, lo).start()

    for off in range(1, Z):
        factor_z(off).wait_recv()

    def scale(j, src):
        at = pl.ds(aligned(j * W), W)
        for part in range(Q):
            for e in range(TOK // SEQ):
                block = cb[j, src, part, e * SEQ : (e + 1) * SEQ, :].astype(f32)
                block = block * fac[src, 2 * part + e : 2 * part + e + 1, :]
                cs[src, pl.ds(part * TOK + e * SEQ, SEQ), at] = block.astype(bf16)

    def scale_near(j, _):
        for off in (0, 1, Z - 1):
            scale(j, lax.rem(z + off, Z))
        return 0

    lax.fori_loop(0, J, scale_near, 0)

    def third_hop(j):
        next_hop(3, j)
        rest_of_third(j)

    def rest_of_third(j):
        hop_plus(5, j).start()
        hop_minus(5, j).start()
        for off in (2, Z - 2):
            scale(j, lax.rem(z + off, Z))

    def third_hops(j, _):
        third_hop(j)
        return 0

    lax.fori_loop(0, AHEAD, third_hops, 0)

    for way in (1, 3):
        y_far(way).wait_recv()
        for lo in range(2):
            x_far(way, lo).wait_recv()
    swap_a(2).start()
    for lo in range(2):
        swap_b(2, lo).start()

    def place(j, part):
        return out_ref.at[:, pl.ds(aligned(part * PART + j * W), W)]

    def give(j, off):
        to = lax.rem(q + off, Q)
        return remote(
            ob.at[j, to], place(j, q), out_s.at[j, off], out_r.at[j, off], q_peer(off)
        )

    def keep(j):
        return pltpu.make_async_copy(ob.at[j, q], place(j, q), own_s.at[j])

    def product(half, j, offs):
        at = pl.ds(aligned(j * W), W)
        grad = acc[half, :, at]
        for off in offs:
            src = lax.rem(z + off, Z)
            grad += jnp.dot(xt[src, half], cs[src, :, at], preferred_element_type=f32)
        return grad

    def multiply_near(half, _):
        grad = jnp.dot(xt[z, half], cs[z], preferred_element_type=f32)
        for off in (1, Z - 1):
            src = lax.rem(z + off, Z)
            grad += jnp.dot(xt[src, half], cs[src], preferred_element_type=f32)
        acc[half] = grad
        return 0

    def multiply_early(j):
        for half in range(2):
            acc[half, :, pl.ds(aligned(j * W), W)] = product(half, j, (2, Z - 2, 3, Z - 3))

    def multiply_late(j):
        hop_plus(4, j).wait_recv()
        hop_minus(4, j).wait_recv()
        scale(j, lax.rem(z + 4, Z))
        for half in range(2):
            grad = product(half, j, (4,)).astype(bf16)
            ob[j, 2 * half] = grad[:OWN]
            ob[j, 2 * half + 1] = grad[OWN:]
        for off in range(1, Q):
            give(j, off).start()
        keep(j).start()

    for off in range(Q):
        swap_a(off).wait_recv()
        for lo in range(2):
            swap_b(off, lo).wait_recv()
    lax.fori_loop(0, 2, multiply_near, 0)

    def last_hops(i, _):
        more = (i >= AHEAD) & (i < J)

        @pl.when(more)
        def _():
            next_hop(3, i)

        @pl.when(i <= J)
        def _():
            next_hop(4, i - 1)

        @pl.when(more)
        def _():
            rest_of_third(i)

        @pl.when(i > 1)
        def _():
            multiply_late(i - 2)

        @pl.when(i <= J)
        def _():
            hop_plus(5, i - 1).wait_recv()
            hop_minus(5, i - 1).wait_recv()
            for off in (3, Z - 3):
                scale(i - 1, lax.rem(z + off, Z))
            multiply_early(i - 1)

        return 0

    lax.fori_loop(1, J + 2, last_hops, 0)

    for off in range(1, Z):
        x_z(off).wait_send()
        factor_z(off).wait_send()
    for off in range(1, T):
        norms(off).wait_send()
    for off in range(1, Q):
        x_a(off).wait_send()
        y_b(off).wait_send()
        factor_q(off).wait_send()
    for off in (1, 3):
        y_a(off).wait_send()
        y_far(off).wait_send()
        for lo in range(2):
            x_b(off, lo).wait_send()
            x_far(off, lo).wait_send()
    for off in range(Q):
        swap_a(off).wait_send()
        for lo in range(2):
            swap_b(off, lo).wait_send()

    def finish(j, _):
        for off in range(1, Q):
            quad(j, off).wait_send()
        for h in range(1, 6):
            hop_plus(h, j).wait_send()
            hop_minus(h, j).wait_send()
        for off in range(1, Q):
            give(j, off).wait_send()
            give(j, off).wait_recv()
        keep(j).wait()
        return 0

    lax.fori_loop(0, J, finish, 0)


def shards(layer_input, gate_pre, up_pre, hidden_cot, other_norms, noise_gate):
    dma = pltpu.SemaphoreType.DMA
    anywhere = pl.BlockSpec(memory_space=pl.ANY)
    grad = pl.pallas_call(
        kernel,
        out_shape=jax.ShapeDtypeStruct((OWN, COLS), bf16),
        in_specs=[anywhere] * 5,
        out_specs=anywhere,
        scratch_shapes=[
            pltpu.VMEM((TOK, D), bf16),
            pltpu.VMEM((TOK, COLS), bf16),
            pltpu.VMEM((TOK, COLS), bf16),
            pltpu.VMEM((TOK, COLS), bf16),
            pltpu.VMEM((2, 16), f32),
            pltpu.VMEM((TOK, COLS), bf16),
            pltpu.VMEM((J, Z, Q, TOK, W), bf16),
            pltpu.VMEM((Z, Q * TOK, PART), bf16),
            pltpu.VMEM((Z, 2, ROWS // 2, Q * TOK), bf16),
            pltpu.VMEM((Z, TOK, TOK), bf16),
            pltpu.VMEM((Z, TOK, TOK), bf16),
            pltpu.VMEM((J, Q, OWN, W), bf16),
            pltpu.VMEM((2, ROWS // 2, PART), f32),
            pltpu.VMEM((2, TOK, TOK), f32),
            pltpu.VMEM((T, 8, 128), f32),
            pltpu.VMEM((Q, 8, 128), f32),
            pltpu.VMEM((Z, 8, 128), f32),
            dma((5,)), dma((Z,)),
            dma((Z,)), dma((Z,)),
            dma((4,)), dma((4,)), dma((4,)), dma((4,)), dma((4,)), dma((4,)),
            dma((2, 4)), dma((2, 4)), dma((4,)), dma((4,)), dma((2, 4)), dma((2, 4)),
            dma((J, Q)), dma((J, Q)),
            dma((5, J)), dma((5, J)), dma((5, J)), dma((5, J)),
            dma((T,)), dma((T,)), dma((Q,)), dma((Q,)), dma((Z,)), dma((Z,)),
            dma((J, Q)), dma((J, Q)), dma((J,)),
        ],
        compiler_params=pltpu.CompilerParams(
            collective_id=0, has_side_effects=True, vmem_limit_bytes=40 * 1024 * 1024
        ),
        cost_estimate=pl.CostEstimate(
            flops=2 * 4096 * 256 * 3584, bytes_accessed=8 * 1024 * 1024, transcendentals=128 * 3584
        ),
        name="clipped_gradient",
    )(*(pltpu.with_memory_space_constraint(a, pltpu.HBM) for a in (layer_input, gate_pre, up_pre, hidden_cot, other_norms)))
    return grad.astype(f32) + noise_gate.astype(f32)


def solution(mesh):
    placed = (
        P("dp", None),
        P("dp", "tensor"),
        P("dp", "tensor"),
        P("dp", "tensor"),
        P("dp", "tensor"),
        P("dp", "tensor"),
    )
    return jax.shard_map(
        shards, mesh=mesh, in_specs=placed, out_specs=P("dp", "tensor"), check_vma=False
    )
```

```python
import math

import jax
import jax.numpy as jnp
from jax import lax
from jax.experimental import pallas as pl
from jax.experimental.pallas import tpu as pltpu
from jax.sharding import PartitionSpec as P

D = 8192
FF = 28672
SEQ = 64
clip_ratio = 0.045
clip_bound = clip_ratio * math.sqrt(SEQ * D * FF)

Z = 8
Q = 4
XN = 4
T = 8
TOK = 128
COLS = 3584
PART = COLS // Q
W = 128
J = PART // W
ROWS = 1024
OWN = ROWS // Q
A, B = pl.ds(0, Z // 2), pl.ds(Z // 2, Z // 2)
AHEAD = 2
MESH = pl.DeviceIdType.MESH
f32 = jnp.float32
bf16 = jnp.bfloat16


def aligned(value, to=128):
    return pl.multiple_of(value, to)


def tokens(q):
    return pl.ds(aligned(q * TOK), TOK)


def kernel(
    x_hbm, g_hbm, u_hbm, c_hbm, other_hbm, out_ref,
    x_v, g_v, u_v, c_v, other_v, gc, cb, cs, xt, xc, xs, ob, acc, gram, pn, fq, fac,
    in_sem, slice_sem, xz_s, xz_r, xa_s, xa_r, yb_s, yb_r, ya_s, ya_r, xb_s, xb_r, ca_s, ca_r, co_s, co_r,
    qa_s, qa_r, rp_s, rp_r, rm_s, rm_r, pn_s, pn_r, fq_s, fq_r, fz_s, fz_r, out_s, out_r, own_s,
):
    dp = lax.axis_index("dp")
    tn = lax.axis_index("tensor")
    z, q = lax.div(dp, Q), lax.rem(dp, Q)
    ylo, core = lax.div(q, 2), lax.rem(q, 2)
    x, yhi = lax.div(tn, 2), lax.rem(tn, 2)
    yy = yhi * 2 + ylo
    xrow = aligned(x * TOK)

    def zq(zd, qd):
        return (zd * Q + qd, tn)

    def x_peer(off):
        return (dp, lax.rem(x + off, XN) * 2 + yhi)

    def y_peer(off):
        to = lax.rem(yy + off, 4)
        return (z * Q + lax.rem(to, 2) * 2 + core, x * 2 + lax.div(to, 2))

    def z_peer(off):
        return zq(lax.rem(z + off, Z), q)

    def q_peer(off):
        return zq(z, lax.rem(q + off, Q))

    def t_peer(off):
        return (dp, lax.rem(tn + off, T))

    core_peer = zq(z, ylo * 2 + 1 - core)

    def remote(src, dst, send, recv, device):
        return pltpu.make_async_remote_copy(
            src_ref=src, dst_ref=dst, send_sem=send, recv_sem=recv,
            device_id=device, device_id_type=MESH,
        )

    loads = [
        pltpu.make_async_copy(src, dst, in_sem.at[i])
        for i, (src, dst) in enumerate(
            ((g_hbm, g_v), (u_hbm, u_v), (c_hbm, c_v), (x_hbm, x_v), (other_hbm, other_v))
        )
    ]

    def slice_of(zd):
        at = pl.ds(aligned(zd * ROWS + yhi * (ROWS // 2) + x * TOK), TOK)
        return pltpu.make_async_copy(x_hbm.at[:, at], xc.at[zd], slice_sem.at[zd])

    for zd in range(Z):
        slice_of(zd).start()
    for load in loads:
        load.start()

    barrier = pltpu.get_barrier_semaphore()

    def greet(device):
        pl.semaphore_signal(barrier, inc=1, device_id=device, device_id_type=MESH)

    for off in range(1, Q):
        greet(q_peer(off))
    for off in range(1, Z):
        greet(z_peer(off))
    for off in range(1, T):
        greet(t_peer(off))
    greet((z * Q + (1 - ylo) * 2 + core, x * 2 + 1 - yhi))

    def quad(j, off):
        to = lax.rem(q + off, Q)
        return remote(
            gc.at[:, pl.ds(aligned(to * PART + j * W), W)], cb.at[j, z, q],
            qa_s.at[j, off], qa_r.at[j, off], q_peer(off),
        )

    def cotangents(j):
        for part in range(Q):
            at = pl.ds(aligned(part * PART + j * W), W)
            gate = g_v[:, at].astype(f32)
            upper = u_v[:, at].astype(f32)
            cotan = c_v[:, at].astype(f32)
            sig = jax.nn.sigmoid(gate)
            slope = sig * (1.0 + gate * (1.0 - sig))
            gc[:, at] = (cotan * upper * slope).astype(bf16)

    def spread(j):
        for off in range(1, Q):
            quad(j, off).start()
        cb[j, z, q] = gc[:, pl.ds(aligned(q * PART + j * W), W)]

    def hop_plus(h, j):
        src = lax.rem(z + Z - {1: 0, 2: 1, 3: 2, 4: 3, 5: 2}[h], Z)
        block = cb.at[j, src]
        if h > 2:
            block = cb.at[j, src, pl.ds(2 if h == 5 else 0, 2)]
        return remote(block, block, rp_s.at[h - 1, j], rp_r.at[h - 1, j], z_peer(1))

    def hop_minus(h, j):
        src = lax.rem(z + {1: 0, 2: 1, 3: 2, 4: 3, 5: 2}[h], Z)
        block = cb.at[j, src]
        if h > 2:
            block = cb.at[j, src, pl.ds(0 if h == 5 else 2, 2)]
        return remote(block, block, rm_s.at[h - 1, j], rm_r.at[h - 1, j], z_peer(Z - 1))

    def first_hop(j):
        for off in range(1, Q):
            quad(j, off).wait_recv()
        hop_plus(1, j).start()
        hop_minus(1, j).start()

    def next_hop(h, j):
        hop_plus(h - 1, j).wait_recv()
        hop_plus(h, j).start()
        hop_minus(h - 1, j).wait_recv()
        hop_minus(h, j).start()

    def turn(zd, _):
        xs[zd] = xc[zd].T
        return 0

    mine = xt.at[z, yhi, pl.ds(xrow, TOK), tokens(q)]

    def x_z(off):
        return remote(xs.at[lax.rem(z + off, Z)], mine, xz_s.at[off], xz_r.at[off], z_peer(off))

    for zd in range(Z):
        slice_of(zd).wait()
    lax.fori_loop(0, Z, turn, 0)
    mine[...] = xs[z]
    pl.semaphore_wait(barrier, (Q - 1) + (Z - 1) + (T - 1) + 1)
    for off in (4, 3, 5, 2, 6, 1, 7):
        x_z(off).start()
    for load in loads[:3]:
        load.wait()
    cotangents(0)
    spread(0)
    cotangents(1)
    first_hop(0)
    spread(1)

    def produce(j, _):
        cotangents(j)
        spread(j)
        first_hop(j - 1)
        return 0

    lax.fori_loop(2, J, produce, 0)
    first_hop(J - 1)

    def x_a(off):
        part = xt.at[A, yhi, pl.ds(xrow, TOK), tokens(q)]
        return remote(part, part, xa_s.at[off], xa_r.at[off], x_peer(off))

    def y_b(off):
        part = xt.at[B, yhi, pl.ds(xrow, TOK), tokens(q)]
        return remote(part, part, yb_s.at[off], yb_r.at[off], y_peer(off))

    def y_a(off):
        part = xt.at[A, yhi, :, tokens(q)]
        return remote(part, part, ya_s.at[off], ya_r.at[off], y_peer(off))

    def x_b(off, lo):
        part = xt.at[B, :, pl.ds(xrow, TOK), tokens(lo * 2 + core)]
        return remote(part, part, xb_s.at[lo, off], xb_r.at[lo, off], x_peer(off))

    def y_far(way):
        src = lax.rem(yy + 4 - way, 4)
        hi, lo = lax.div(src, 2), lax.rem(src, 2)
        at = pl.ds(0 if way == 1 else 2, 2)
        part = xt.at[at, hi, :, tokens(lo * 2 + core)]
        return remote(part, part, ya_s.at[way - 1], ya_r.at[way - 1], y_peer(way))

    def x_far(way, lo):
        row = aligned(lax.rem(x + XN - way, XN) * TOK)
        at = pl.ds(4 if way == 1 else 6, 2)
        part = xt.at[at, :, pl.ds(row, TOK), tokens(lo * 2 + core)]
        return remote(part, part, xb_s.at[lo, way - 1], xb_r.at[lo, way - 1], x_peer(way))

    def swap_a(off):
        src = lax.rem(yy + off, 4)
        hi, lo = lax.div(src, 2), lax.rem(src, 2)
        part = xt.at[A, hi, :, tokens(lo * 2 + core)]
        return remote(part, part, ca_s.at[off], ca_r.at[off], core_peer)

    def swap_b(off, lo):
        row = aligned(lax.rem(x + off, XN) * TOK)
        part = xt.at[B, :, pl.ds(row, TOK), tokens(lo * 2 + core)]
        return remote(part, part, co_s.at[lo, off], co_r.at[lo, off], core_peer)

    for off in range(1, Z):
        x_z(off).wait_recv()
    for off in range(1, XN):
        x_a(off).start()
        y_b(off).start()

    cross = (((1,), (1,)), ((), ()))
    gram[...] = jnp.zeros_like(gram)
    loads[3].wait()
    loads[4].wait()

    def gram_x(k, _):
        part = x_v[:, pl.ds(aligned(k * 1024), 1024)]
        gram[0] += lax.dot_general(part, part, cross, preferred_element_type=f32)
        return 0

    lax.fori_loop(0, D // 1024, gram_x, 0)

    def gram_cot(k, _):
        at = pl.ds(aligned(k * 512), 512)
        gate = g_v[:, at].astype(f32)
        upper = (c_v[:, at].astype(f32) * (gate * jax.nn.sigmoid(gate))).astype(bf16)
        gate = gc[:, at]
        gram[1] += lax.dot_general(
            gate, gate, cross, preferred_element_type=f32
        ) + lax.dot_general(upper, upper, cross, preferred_element_type=f32)
        return 0

    lax.fori_loop(0, COLS // 512, gram_cot, 0)

    for e in range(TOK // SEQ):
        at = slice(e * SEQ, (e + 1) * SEQ)
        ghost = jnp.sum(gram[0, at, at] * gram[1, at, at], axis=1, keepdims=True)
        ghost = jnp.sum(ghost, axis=0, keepdims=True)
        rest = jnp.sum(other_v[e : e + 1, :], axis=1, keepdims=True)
        pn[0, e : e + 1, :] = jnp.broadcast_to(ghost + rest, (1, 128))
    pn[0, 2:8, :] = jnp.zeros((6, 128), f32)

    def norms(off):
        return remote(pn.at[0], pn.at[off], pn_s.at[off], pn_r.at[off], t_peer(off))

    for off in range(1, T):
        norms(off).start()

    def factor_q(off):
        return remote(fq.at[q], fq.at[q], fq_s.at[off], fq_r.at[off], q_peer(off))

    def factor_z(off):
        return remote(fac.at[z], fac.at[z], fz_s.at[off], fz_r.at[off], z_peer(off))

    def second_hop(j, _):
        next_hop(2, j)
        return 0

    for off in range(1, XN):
        y_b(off).wait_recv()
    for off in (1, 3):
        for lo in range(2):
            x_b(off, lo).start()
    lax.fori_loop(0, 1, second_hop, 0)

    for off in range(1, T):
        norms(off).wait_recv()
    total = jnp.zeros((8, 128), f32)
    for t in range(T):
        total = total + pn[lax.rem(tn + T - t, T)]
    fq[q] = clip_bound / jnp.maximum(jnp.sqrt(total), clip_bound)
    for off in range(1, Q):
        factor_q(off).start()

    for off in range(1, XN):
        x_a(off).wait_recv()
    for off in (1, 3):
        y_a(off).start()
    swap_a(0).start()
    for lo in range(2):
        swap_b(0, lo).start()
    for off in range(1, Q):
        factor_q(off).wait_recv()
    for part in range(Q):
        fac[z, 2 * part : 2 * part + 2, :] = fq[part, 0:2, :]
    for off in range(1, Z):
        factor_z(off).start()

    lax.fori_loop(1, J, second_hop, 0)

    for off in (1, 3):
        y_a(off).wait_recv()
        y_far(off).start()
        for lo in range(2):
            x_b(off, lo).wait_recv()
            x_far(off, lo).start()
        swap_a(4 - off).start()
        for lo in range(2):
            swap_b(4 - off, lo).start()

    def rest_of_third(j):
        hop_plus(5, j).start()
        hop_minus(5, j).start()

    def third_hops(j, _):
        next_hop(3, j)
        rest_of_third(j)
        return 0

    lax.fori_loop(0, AHEAD, third_hops, 0)

    for off in range(1, Z):
        factor_z(off).wait_recv()

    def scale(j, src):
        at = pl.ds(aligned(j * W), W)
        for part in range(Q):
            for e in range(TOK // SEQ):
                block = cb[j, src, part, e * SEQ : (e + 1) * SEQ, :].astype(f32)
                block = block * fac[src, 2 * part + e : 2 * part + e + 1, :]
                cs[src, pl.ds(part * TOK + e * SEQ, SEQ), at] = block.astype(bf16)

    def scale_near(j, _):
        for off in (0, 1, Z - 1):
            scale(j, lax.rem(z + off, Z))
        return 0

    lax.fori_loop(0, J, scale_near, 0)

    def scale_second(j):
        for off in (2, Z - 2):
            scale(j, lax.rem(z + off, Z))

    def scale_seconds(j, _):
        scale_second(j)
        return 0

    lax.fori_loop(0, AHEAD, scale_seconds, 0)

    for way in (1, 3):
        y_far(way).wait_recv()
        for lo in range(2):
            x_far(way, lo).wait_recv()
    swap_a(2).start()
    for lo in range(2):
        swap_b(2, lo).start()

    def place(j, part):
        return out_ref.at[:, pl.ds(aligned(part * PART + j * W), W)]

    def give(j, off):
        to = lax.rem(q + off, Q)
        return remote(
            ob.at[j, to], place(j, q), out_s.at[j, off], out_r.at[j, off], q_peer(off)
        )

    def keep(j):
        return pltpu.make_async_copy(ob.at[j, q], place(j, q), own_s.at[j])

    def product(half, j, offs):
        at = pl.ds(aligned(j * W), W)
        grad = acc[half, :, at]
        for off in offs:
            src = lax.rem(z + off, Z)
            grad += jnp.dot(xt[src, half], cs[src, :, at], preferred_element_type=f32)
        return grad

    def multiply_near(half, _):
        grad = jnp.dot(xt[z, half], cs[z], preferred_element_type=f32)
        for off in (1, Z - 1):
            src = lax.rem(z + off, Z)
            grad += jnp.dot(xt[src, half], cs[src], preferred_element_type=f32)
        acc[half] = grad
        return 0

    def multiply_early(j):
        for half in range(2):
            acc[half, :, pl.ds(aligned(j * W), W)] = product(half, j, (2, Z - 2, 3, Z - 3))

    def multiply_late(j):
        hop_plus(4, j).wait_recv()
        hop_minus(4, j).wait_recv()
        scale(j, lax.rem(z + 4, Z))
        for half in range(2):
            grad = product(half, j, (4,)).astype(bf16)
            ob[j, 2 * half] = grad[:OWN]
            ob[j, 2 * half + 1] = grad[OWN:]
        for off in range(1, Q):
            give(j, off).start()
        keep(j).start()

    for off in range(Q):
        swap_a(off).wait_recv()
        for lo in range(2):
            swap_b(off, lo).wait_recv()
    lax.fori_loop(0, 2, multiply_near, 0)

    def last_hops(i, _):
        more = (i >= AHEAD) & (i < J)

        @pl.when(more)
        def _():
            next_hop(3, i)

        @pl.when(i <= J)
        def _():
            next_hop(4, i - 1)

        @pl.when(more)
        def _():
            rest_of_third(i)
            scale_second(i)

        @pl.when(i > 1)
        def _():
            multiply_late(i - 2)

        @pl.when(i <= J)
        def _():
            hop_plus(5, i - 1).wait_recv()
            hop_minus(5, i - 1).wait_recv()
            for off in (3, Z - 3):
                scale(i - 1, lax.rem(z + off, Z))
            multiply_early(i - 1)

        return 0

    lax.fori_loop(1, J + 2, last_hops, 0)

    for off in range(1, Z):
        x_z(off).wait_send()
        factor_z(off).wait_send()
    for off in range(1, T):
        norms(off).wait_send()
    for off in range(1, Q):
        x_a(off).wait_send()
        y_b(off).wait_send()
        factor_q(off).wait_send()
    for off in (1, 3):
        y_a(off).wait_send()
        y_far(off).wait_send()
        for lo in range(2):
            x_b(off, lo).wait_send()
            x_far(off, lo).wait_send()
    for off in range(Q):
        swap_a(off).wait_send()
        for lo in range(2):
            swap_b(off, lo).wait_send()

    def finish(j, _):
        for off in range(1, Q):
            quad(j, off).wait_send()
        for h in range(1, 6):
            hop_plus(h, j).wait_send()
            hop_minus(h, j).wait_send()
        for off in range(1, Q):
            give(j, off).wait_send()
            give(j, off).wait_recv()
        keep(j).wait()
        return 0

    lax.fori_loop(0, J, finish, 0)


def shards(layer_input, gate_pre, up_pre, hidden_cot, other_norms, noise_gate):
    dma = pltpu.SemaphoreType.DMA
    anywhere = pl.BlockSpec(memory_space=pl.ANY)
    grad = pl.pallas_call(
        kernel,
        out_shape=jax.ShapeDtypeStruct((OWN, COLS), bf16),
        in_specs=[anywhere] * 5,
        out_specs=anywhere,
        scratch_shapes=[
            pltpu.VMEM((TOK, D), bf16),
            pltpu.VMEM((TOK, COLS), bf16),
            pltpu.VMEM((TOK, COLS), bf16),
            pltpu.VMEM((TOK, COLS), bf16),
            pltpu.VMEM((2, 16), f32),
            pltpu.VMEM((TOK, COLS), bf16),
            pltpu.VMEM((J, Z, Q, TOK, W), bf16),
            pltpu.VMEM((Z, Q * TOK, PART), bf16),
            pltpu.VMEM((Z, 2, ROWS // 2, Q * TOK), bf16),
            pltpu.VMEM((Z, TOK, TOK), bf16),
            pltpu.VMEM((Z, TOK, TOK), bf16),
            pltpu.VMEM((J, Q, OWN, W), bf16),
            pltpu.VMEM((2, ROWS // 2, PART), f32),
            pltpu.VMEM((2, TOK, TOK), f32),
            pltpu.VMEM((T, 8, 128), f32),
            pltpu.VMEM((Q, 8, 128), f32),
            pltpu.VMEM((Z, 8, 128), f32),
            dma((5,)), dma((Z,)),
            dma((Z,)), dma((Z,)),
            dma((4,)), dma((4,)), dma((4,)), dma((4,)), dma((4,)), dma((4,)),
            dma((2, 4)), dma((2, 4)), dma((4,)), dma((4,)), dma((2, 4)), dma((2, 4)),
            dma((J, Q)), dma((J, Q)),
            dma((5, J)), dma((5, J)), dma((5, J)), dma((5, J)),
            dma((T,)), dma((T,)), dma((Q,)), dma((Q,)), dma((Z,)), dma((Z,)),
            dma((J, Q)), dma((J, Q)), dma((J,)),
        ],
        compiler_params=pltpu.CompilerParams(
            collective_id=0, has_side_effects=True, vmem_limit_bytes=40 * 1024 * 1024
        ),
        cost_estimate=pl.CostEstimate(
            flops=2 * 4096 * 256 * 3584, bytes_accessed=8 * 1024 * 1024, transcendentals=128 * 3584
        ),
        name="clipped_gradient",
    )(*(pltpu.with_memory_space_constraint(a, pltpu.HBM) for a in (layer_input, gate_pre, up_pre, hidden_cot, other_norms)))
    return grad.astype(f32) + noise_gate.astype(f32)


def solution(mesh):
    placed = (
        P("dp", None),
        P("dp", "tensor"),
        P("dp", "tensor"),
        P("dp", "tensor"),
        P("dp", "tensor"),
        P("dp", "tensor"),
    )
    return jax.shard_map(
        shards, mesh=mesh, in_specs=placed, out_specs=P("dp", "tensor"), check_vma=False
    )
```

```python
import math

import jax
import jax.numpy as jnp
from jax import lax
from jax.experimental import pallas as pl
from jax.experimental.pallas import tpu as pltpu
from jax.sharding import PartitionSpec as P

D = 8192
FF = 28672
SEQ = 64
clip_ratio = 0.045
clip_bound = clip_ratio * math.sqrt(SEQ * D * FF)

Z = 8
Q = 4
XN = 4
T = 8
TOK = 128
COLS = 3584
PART = COLS // Q
W = 128
J = PART // W
ROWS = 1024
OWN = ROWS // Q
A, B = pl.ds(0, Z // 2), pl.ds(Z // 2, Z // 2)
AHEAD = 2
MESH = pl.DeviceIdType.MESH
f32 = jnp.float32
bf16 = jnp.bfloat16


def aligned(value, to=128):
    return pl.multiple_of(value, to)


def tokens(q):
    return pl.ds(aligned(q * TOK), TOK)


def kernel(
    x_hbm, g_hbm, u_hbm, c_hbm, other_hbm, out_ref,
    x_v, g_v, u_v, c_v, other_v, gc, cb, cs, xt, xc, xs, ob, acc, gram, pn, fq, fac,
    in_sem, slice_sem, xz_s, xz_r, xa_s, xa_r, yb_s, yb_r, ya_s, ya_r, xb_s, xb_r, ca_s, ca_r, co_s, co_r,
    qa_s, qa_r, rp_s, rp_r, rm_s, rm_r, pn_s, pn_r, fq_s, fq_r, fz_s, fz_r, out_s, out_r, own_s,
):
    dp = lax.axis_index("dp")
    tn = lax.axis_index("tensor")
    z, q = lax.div(dp, Q), lax.rem(dp, Q)
    ylo, core = lax.div(q, 2), lax.rem(q, 2)
    x, yhi = lax.div(tn, 2), lax.rem(tn, 2)
    yy = yhi * 2 + ylo
    xrow = aligned(x * TOK)

    def zq(zd, qd):
        return (zd * Q + qd, tn)

    def x_peer(off):
        return (dp, lax.rem(x + off, XN) * 2 + yhi)

    def y_peer(off):
        to = lax.rem(yy + off, 4)
        return (z * Q + lax.rem(to, 2) * 2 + core, x * 2 + lax.div(to, 2))

    def z_peer(off):
        return zq(lax.rem(z + off, Z), q)

    def q_peer(off):
        return zq(z, lax.rem(q + off, Q))

    def t_peer(off):
        return (dp, lax.rem(tn + off, T))

    core_peer = zq(z, ylo * 2 + 1 - core)

    def remote(src, dst, send, recv, device):
        return pltpu.make_async_remote_copy(
            src_ref=src, dst_ref=dst, send_sem=send, recv_sem=recv,
            device_id=device, device_id_type=MESH,
        )

    loads = [
        pltpu.make_async_copy(src, dst, in_sem.at[i])
        for i, (src, dst) in enumerate(
            ((g_hbm, g_v), (u_hbm, u_v), (c_hbm, c_v), (x_hbm, x_v), (other_hbm, other_v))
        )
    ]

    def slice_of(zd):
        at = pl.ds(aligned(zd * ROWS + yhi * (ROWS // 2) + x * TOK), TOK)
        return pltpu.make_async_copy(x_hbm.at[:, at], xc.at[zd], slice_sem.at[zd])

    for zd in range(Z):
        slice_of(zd).start()
    for load in loads:
        load.start()

    barrier = pltpu.get_barrier_semaphore()

    def greet(device):
        pl.semaphore_signal(barrier, inc=1, device_id=device, device_id_type=MESH)

    for off in range(1, Q):
        greet(q_peer(off))
    for off in range(1, Z):
        greet(z_peer(off))
    for off in range(1, T):
        greet(t_peer(off))
    greet((z * Q + (1 - ylo) * 2 + core, x * 2 + 1 - yhi))

    def quad(j, off):
        to = lax.rem(q + off, Q)
        return remote(
            gc.at[:, pl.ds(aligned(to * PART + j * W), W)], cb.at[j, z, q],
            qa_s.at[j, off], qa_r.at[j, off], q_peer(off),
        )

    def cotangents(j):
        for part in range(Q):
            at = pl.ds(aligned(part * PART + j * W), W)
            gate = g_v[:, at].astype(f32)
            upper = u_v[:, at].astype(f32)
            cotan = c_v[:, at].astype(f32)
            sig = jax.nn.sigmoid(gate)
            slope = sig * (1.0 + gate * (1.0 - sig))
            gc[:, at] = (cotan * upper * slope).astype(bf16)

    def spread(j):
        for off in range(1, Q):
            quad(j, off).start()
        cb[j, z, q] = gc[:, pl.ds(aligned(q * PART + j * W), W)]

    def hop_plus(h, j):
        src = lax.rem(z + Z - {1: 0, 2: 1, 3: 2, 4: 3, 5: 2}[h], Z)
        block = cb.at[j, src]
        if h > 2:
            block = cb.at[j, src, pl.ds(2 if h == 5 else 0, 2)]
        return remote(block, block, rp_s.at[h - 1, j], rp_r.at[h - 1, j], z_peer(1))

    def hop_minus(h, j):
        src = lax.rem(z + {1: 0, 2: 1, 3: 2, 4: 3, 5: 2}[h], Z)
        block = cb.at[j, src]
        if h > 2:
            block = cb.at[j, src, pl.ds(0 if h == 5 else 2, 2)]
        return remote(block, block, rm_s.at[h - 1, j], rm_r.at[h - 1, j], z_peer(Z - 1))

    def first_hop(j):
        for off in range(1, Q):
            quad(j, off).wait_recv()
        hop_plus(1, j).start()
        hop_minus(1, j).start()

    def next_hop(h, j):
        hop_plus(h - 1, j).wait_recv()
        hop_plus(h, j).start()
        hop_minus(h - 1, j).wait_recv()
        hop_minus(h, j).start()

    def turn(zd, _):
        xs[zd] = xc[zd].T
        return 0

    mine = xt.at[z, yhi, pl.ds(xrow, TOK), tokens(q)]

    def x_z(off):
        return remote(xs.at[lax.rem(z + off, Z)], mine, xz_s.at[off], xz_r.at[off], z_peer(off))

    for zd in range(Z):
        slice_of(zd).wait()
    lax.fori_loop(0, Z, turn, 0)
    mine[...] = xs[z]
    pl.semaphore_wait(barrier, (Q - 1) + (Z - 1) + (T - 1) + 1)
    for off in (4, 3, 5, 2, 6, 1, 7):
        x_z(off).start()
    for load in loads[:3]:
        load.wait()
    cotangents(0)
    spread(0)
    cotangents(1)
    spread(1)
    first_hop(0)

    def produce(j, _):
        cotangents(j)
        spread(j)
        first_hop(j - 1)
        return 0

    lax.fori_loop(2, J, produce, 0)
    first_hop(J - 1)

    def x_a(off):
        part = xt.at[A, yhi, pl.ds(xrow, TOK), tokens(q)]
        return remote(part, part, xa_s.at[off], xa_r.at[off], x_peer(off))

    def y_b(off):
        part = xt.at[B, yhi, pl.ds(xrow, TOK), tokens(q)]
        return remote(part, part, yb_s.at[off], yb_r.at[off], y_peer(off))

    def y_a(off):
        part = xt.at[A, yhi, :, tokens(q)]
        return remote(part, part, ya_s.at[off], ya_r.at[off], y_peer(off))

    def x_b(off, lo):
        part = xt.at[B, :, pl.ds(xrow, TOK), tokens(lo * 2 + core)]
        return remote(part, part, xb_s.at[lo, off], xb_r.at[lo, off], x_peer(off))

    def y_far(way):
        src = lax.rem(yy + 4 - way, 4)
        hi, lo = lax.div(src, 2), lax.rem(src, 2)
        at = pl.ds(0 if way == 1 else 2, 2)
        part = xt.at[at, hi, :, tokens(lo * 2 + core)]
        return remote(part, part, ya_s.at[way - 1], ya_r.at[way - 1], y_peer(way))

    def x_far(way, lo):
        row = aligned(lax.rem(x + XN - way, XN) * TOK)
        at = pl.ds(4 if way == 1 else 6, 2)
        part = xt.at[at, :, pl.ds(row, TOK), tokens(lo * 2 + core)]
        return remote(part, part, xb_s.at[lo, way - 1], xb_r.at[lo, way - 1], x_peer(way))

    def swap_a(off):
        src = lax.rem(yy + off, 4)
        hi, lo = lax.div(src, 2), lax.rem(src, 2)
        part = xt.at[A, hi, :, tokens(lo * 2 + core)]
        return remote(part, part, ca_s.at[off], ca_r.at[off], core_peer)

    def swap_b(off, lo):
        row = aligned(lax.rem(x + off, XN) * TOK)
        part = xt.at[B, :, pl.ds(row, TOK), tokens(lo * 2 + core)]
        return remote(part, part, co_s.at[lo, off], co_r.at[lo, off], core_peer)

    for off in range(1, Z):
        x_z(off).wait_recv()
    for off in range(1, XN):
        x_a(off).start()
        y_b(off).start()

    cross = (((1,), (1,)), ((), ()))
    gram[...] = jnp.zeros_like(gram)
    loads[3].wait()
    loads[4].wait()

    def gram_x(k, _):
        part = x_v[:, pl.ds(aligned(k * 1024), 1024)]
        gram[0] += lax.dot_general(part, part, cross, preferred_element_type=f32)
        return 0

    lax.fori_loop(0, D // 1024, gram_x, 0)

    def gram_cot(k, _):
        at = pl.ds(aligned(k * 512), 512)
        gate = g_v[:, at].astype(f32)
        upper = (c_v[:, at].astype(f32) * (gate * jax.nn.sigmoid(gate))).astype(bf16)
        gate = gc[:, at]
        gram[1] += lax.dot_general(
            gate, gate, cross, preferred_element_type=f32
        ) + lax.dot_general(upper, upper, cross, preferred_element_type=f32)
        return 0

    lax.fori_loop(0, COLS // 512, gram_cot, 0)

    for e in range(TOK // SEQ):
        at = slice(e * SEQ, (e + 1) * SEQ)
        ghost = jnp.sum(gram[0, at, at] * gram[1, at, at], axis=1, keepdims=True)
        ghost = jnp.sum(ghost, axis=0, keepdims=True)
        rest = jnp.sum(other_v[e : e + 1, :], axis=1, keepdims=True)
        pn[0, e : e + 1, :] = jnp.broadcast_to(ghost + rest, (1, 128))
    pn[0, 2:8, :] = jnp.zeros((6, 128), f32)

    def norms(off):
        return remote(pn.at[0], pn.at[off], pn_s.at[off], pn_r.at[off], t_peer(off))

    for off in range(1, T):
        norms(off).start()

    def factor_q(off):
        return remote(fq.at[q], fq.at[q], fq_s.at[off], fq_r.at[off], q_peer(off))

    def factor_z(off):
        return remote(fac.at[z], fac.at[z], fz_s.at[off], fz_r.at[off], z_peer(off))

    def second_hop(j, _):
        next_hop(2, j)
        return 0

    for off in range(1, XN):
        y_b(off).wait_recv()
    for off in (1, 3):
        for lo in range(2):
            x_b(off, lo).start()
    lax.fori_loop(0, 1, second_hop, 0)

    for off in range(1, T):
        norms(off).wait_recv()
    total = jnp.zeros((8, 128), f32)
    for t in range(T):
        total = total + pn[lax.rem(tn + T - t, T)]
    fq[q] = clip_bound / jnp.maximum(jnp.sqrt(total), clip_bound)
    for off in range(1, Q):
        factor_q(off).start()

    for off in range(1, XN):
        x_a(off).wait_recv()
    for off in (1, 3):
        y_a(off).start()
    swap_a(0).start()
    for lo in range(2):
        swap_b(0, lo).start()
    lax.fori_loop(1, 4, second_hop, 0)

    for off in range(1, Q):
        factor_q(off).wait_recv()
    for part in range(Q):
        fac[z, 2 * part : 2 * part + 2, :] = fq[part, 0:2, :]
    for off in range(1, Z):
        factor_z(off).start()

    lax.fori_loop(4, J, second_hop, 0)

    for off in (1, 3):
        y_a(off).wait_recv()
        y_far(off).start()
        for lo in range(2):
            x_b(off, lo).wait_recv()
            x_far(off, lo).start()
        swap_a(4 - off).start()
        for lo in range(2):
            swap_b(4 - off, lo).start()

    for off in range(1, Z):
        factor_z(off).wait_recv()

    def scale(j, src):
        at = pl.ds(aligned(j * W), W)
        for part in range(Q):
            for e in range(TOK // SEQ):
                block = cb[j, src, part, e * SEQ : (e + 1) * SEQ, :].astype(f32)
                block = block * fac[src, 2 * part + e : 2 * part + e + 1, :]
                cs[src, pl.ds(part * TOK + e * SEQ, SEQ), at] = block.astype(bf16)

    def scale_near(j, _):
        for off in (0, 1, Z - 1):
            scale(j, lax.rem(z + off, Z))
        return 0

    lax.fori_loop(0, J, scale_near, 0)

    def third_hop(j):
        next_hop(3, j)
        rest_of_third(j)

    def rest_of_third(j):
        hop_plus(5, j).start()
        hop_minus(5, j).start()
        for off in (2, Z - 2):
            scale(j, lax.rem(z + off, Z))

    def third_hops(j, _):
        third_hop(j)
        return 0

    lax.fori_loop(0, AHEAD, third_hops, 0)

    for way in (1, 3):
        y_far(way).wait_recv()
        for lo in range(2):
            x_far(way, lo).wait_recv()
    swap_a(2).start()
    for lo in range(2):
        swap_b(2, lo).start()

    def place(j, part):
        return out_ref.at[:, pl.ds(aligned(part * PART + j * W), W)]

    def give(j, off):
        to = lax.rem(q + off, Q)
        return remote(
            ob.at[j, to], place(j, q), out_s.at[j, off], out_r.at[j, off], q_peer(off)
        )

    def keep(j):
        return pltpu.make_async_copy(ob.at[j, q], place(j, q), own_s.at[j])

    def product(half, j, offs):
        at = pl.ds(aligned(j * W), W)
        grad = acc[half, :, at]
        for off in offs:
            src = lax.rem(z + off, Z)
            grad += jnp.dot(xt[src, half], cs[src, :, at], preferred_element_type=f32)
        return grad

    def multiply_near(half, _):
        grad = jnp.dot(xt[z, half], cs[z], preferred_element_type=f32)
        for off in (1, Z - 1):
            src = lax.rem(z + off, Z)
            grad += jnp.dot(xt[src, half], cs[src], preferred_element_type=f32)
        acc[half] = grad
        return 0

    def multiply_early(j):
        for half in range(2):
            acc[half, :, pl.ds(aligned(j * W), W)] = product(half, j, (2, Z - 2, 3, Z - 3))

    def multiply_late(j):
        hop_plus(4, j).wait_recv()
        hop_minus(4, j).wait_recv()
        scale(j, lax.rem(z + 4, Z))
        for half, offs in ((1 - ylo, (2, 3 - 2 * core)), (ylo, (1 + 2 * core,))):
            grad = product(half, j, (4,)).astype(bf16)
            ob[j, 2 * half] = grad[:OWN]
            ob[j, 2 * half + 1] = grad[OWN:]
            for off in offs:
                give(j, off).start()
        keep(j).start()

    for off in range(Q):
        swap_a(off).wait_recv()
        for lo in range(2):
            swap_b(off, lo).wait_recv()
    lax.fori_loop(0, 2, multiply_near, 0)

    def last_hops(i, _):
        more = (i >= AHEAD) & (i < J)

        @pl.when(more)
        def _():
            next_hop(3, i)

        @pl.when(i <= J)
        def _():
            next_hop(4, i - 1)

        @pl.when(more)
        def _():
            rest_of_third(i)

        @pl.when(i > 1)
        def _():
            multiply_late(i - 2)

        @pl.when(i <= J)
        def _():
            hop_plus(5, i - 1).wait_recv()
            hop_minus(5, i - 1).wait_recv()
            for off in (3, Z - 3):
                scale(i - 1, lax.rem(z + off, Z))
            multiply_early(i - 1)

        return 0

    lax.fori_loop(1, J + 2, last_hops, 0)

    for off in range(1, Z):
        x_z(off).wait_send()
        factor_z(off).wait_send()
    for off in range(1, T):
        norms(off).wait_send()
    for off in range(1, Q):
        x_a(off).wait_send()
        y_b(off).wait_send()
        factor_q(off).wait_send()
    for off in (1, 3):
        y_a(off).wait_send()
        y_far(off).wait_send()
        for lo in range(2):
            x_b(off, lo).wait_send()
            x_far(off, lo).wait_send()
    for off in range(Q):
        swap_a(off).wait_send()
        for lo in range(2):
            swap_b(off, lo).wait_send()

    def finish(j, _):
        for off in range(1, Q):
            quad(j, off).wait_send()
        for h in range(1, 6):
            hop_plus(h, j).wait_send()
            hop_minus(h, j).wait_send()
        for off in range(1, Q):
            give(j, off).wait_send()
            give(j, off).wait_recv()
        keep(j).wait()
        return 0

    lax.fori_loop(0, J, finish, 0)


def shards(layer_input, gate_pre, up_pre, hidden_cot, other_norms, noise_gate):
    dma = pltpu.SemaphoreType.DMA
    anywhere = pl.BlockSpec(memory_space=pl.ANY)
    grad = pl.pallas_call(
        kernel,
        out_shape=jax.ShapeDtypeStruct((OWN, COLS), bf16),
        in_specs=[anywhere] * 5,
        out_specs=anywhere,
        scratch_shapes=[
            pltpu.VMEM((TOK, D), bf16),
            pltpu.VMEM((TOK, COLS), bf16),
            pltpu.VMEM((TOK, COLS), bf16),
            pltpu.VMEM((TOK, COLS), bf16),
            pltpu.VMEM((2, 16), f32),
            pltpu.VMEM((TOK, COLS), bf16),
            pltpu.VMEM((J, Z, Q, TOK, W), bf16),
            pltpu.VMEM((Z, Q * TOK, PART), bf16),
            pltpu.VMEM((Z, 2, ROWS // 2, Q * TOK), bf16),
            pltpu.VMEM((Z, TOK, TOK), bf16),
            pltpu.VMEM((Z, TOK, TOK), bf16),
            pltpu.VMEM((J, Q, OWN, W), bf16),
            pltpu.VMEM((2, ROWS // 2, PART), f32),
            pltpu.VMEM((2, TOK, TOK), f32),
            pltpu.VMEM((T, 8, 128), f32),
            pltpu.VMEM((Q, 8, 128), f32),
            pltpu.VMEM((Z, 8, 128), f32),
            dma((5,)), dma((Z,)),
            dma((Z,)), dma((Z,)),
            dma((4,)), dma((4,)), dma((4,)), dma((4,)), dma((4,)), dma((4,)),
            dma((2, 4)), dma((2, 4)), dma((4,)), dma((4,)), dma((2, 4)), dma((2, 4)),
            dma((J, Q)), dma((J, Q)),
            dma((5, J)), dma((5, J)), dma((5, J)), dma((5, J)),
            dma((T,)), dma((T,)), dma((Q,)), dma((Q,)), dma((Z,)), dma((Z,)),
            dma((J, Q)), dma((J, Q)), dma((J,)),
        ],
        compiler_params=pltpu.CompilerParams(
            collective_id=0, has_side_effects=True, vmem_limit_bytes=40 * 1024 * 1024
        ),
        cost_estimate=pl.CostEstimate(
            flops=2 * 4096 * 256 * 3584, bytes_accessed=8 * 1024 * 1024, transcendentals=128 * 3584
        ),
        name="clipped_gradient",
    )(*(pltpu.with_memory_space_constraint(a, pltpu.HBM) for a in (layer_input, gate_pre, up_pre, hidden_cot, other_norms)))
    return grad.astype(f32) + noise_gate.astype(f32)


def solution(mesh):
    placed = (
        P("dp", None),
        P("dp", "tensor"),
        P("dp", "tensor"),
        P("dp", "tensor"),
        P("dp", "tensor"),
        P("dp", "tensor"),
    )
    return jax.shard_map(
        shards, mesh=mesh, in_specs=placed, out_specs=P("dp", "tensor"), check_vma=False
    )
```
